256 devices in a mesh: grp: 16 (over y_hi, x, core), tok: 16 (over y_lo, z).
Axes of the slice: x: 4, y: 4 (y_hi: 2, y_lo: 2; y = y_hi * 2 + y_lo), z: 8, core: 2. Of those that a mesh axis runs over, the one named last changes fastest.
Arguments:
- tokens: bfloat16 [16, 2048, 4096], P('grp', 'tok'), may hold values from -6 to 6
- modulation: float32 [2, 4096], replicated, may hold values from -3 to 3
- triple_weight: bfloat16 [4096, 3, 2048], P(None, None, 'tok'), may hold values from -2.25 to 2.25
- out_weight: bfloat16 [2048, 4096], P(None, 'tok'), may hold values from -0.125 to 0.125
- gate: float32 [4096], P('tok'), may hold values from -8 to 8
- latent_weight: bfloat16 [4096, 128], replicated, may hold values from -0.09375 to 0.09375
- conv_weight: bfloat16 [3, 3, 3, 128, 256], replicated, may hold values from -0.109375 to 0.109375
- conv_bias: float32 [256], replicated, may hold values from -3 to 3
- res_weight: bfloat16 [3, 3, 3, 256, 256], replicated, may hold values from -0.078125 to 0.078125
- res_bias: float32 [256], replicated, may hold values from -3 to 3
Outputs:
- upsampled: bfloat16 [16, 128, 64, 256], P(None, 'grp', 'tok')
The draws below stay inside these ranges and needn't reach their ends.
All inputs are finite; a program needn't handle non-finite values.
Results may differ from the reference program's by a relative error of at most 0.018.
Values may be sent and summed in bfloat16 or wider, within the bound.
A program may use at most 128 MiB of HBM per device.

```python
import jax
import jax.numpy as jnp
from jax import lax

D = 4096
HEADS = 16
HEAD_DIM = 128
LAT = 128
CH = 256
HB = 4
FRAMES = 16
WW = 32
REGIONS = 16
HH = 64
SEQ = 2048


def draw_tokens(key, part):
    key = jax.random.fold_in(key, 11)
    values = jax.random.normal(key, (REGIONS, SEQ, D), jnp.float32)
    return jnp.clip(values, -6.0, 6.0).astype(jnp.bfloat16)


def draw_triple_weight(key, part):
    key = jax.random.fold_in(key, 12)
    base = jnp.clip(jax.random.normal(key, (D, 3, HEADS * HEAD_DIM), jnp.float32), -6.0, 6.0) * D ** (-0.5)
    return base.astype(jnp.bfloat16)


def level_of(key, extent, pieces, low, largest):
    level = 1.0
    for axis_at, parts in pieces:
        steps = jax.random.uniform(jax.random.fold_in(jax.random.fold_in(key, 6), axis_at), (parts,), jnp.float32, low / len(pieces), largest / len(pieces))
        level = level * jnp.repeat(jnp.exp(steps), extent[axis_at] // parts).reshape((-1,) + (1,) * (len(extent) - 1 - axis_at))
    return level


def bell_draw(rng, shape, width, reach, cuts=(), kind=jnp.bfloat16):
    drawn = jax.random.normal(rng, shape, jnp.float32) * width
    if len(cuts) > 0:
        drawn = level_of(rng, shape, cuts, -0.22, 0.18) * drawn
    return jnp.clip(drawn, min=-reach, max=reach).astype(kind)


def setup_inputs(seed: int = 0) -> dict:
    seeds = jax.random.split(jax.random.key(seed), 11)
    return {
        "tokens": draw_tokens(jax.random.fold_in(seeds[10], 71), 0),
        "modulation": bell_draw(seeds[1], (2, D), 0.5, 3.0, (), jnp.float32),
        "triple_weight": draw_triple_weight(jax.random.fold_in(seeds[10], 71), 0),
        "out_weight": bell_draw(seeds[3], (HEADS * HEAD_DIM, D), (HEADS * HEAD_DIM) ** -0.5, 0.125, ((1, 16),)),
        "gate": bell_draw(seeds[4], (D,), 2.0, 8.0, ((0, 16),), jnp.float32),
        "latent_weight": bell_draw(seeds[5], (D, LAT), D ** -0.5, 0.09375),
        "conv_weight": bell_draw(seeds[6], (3, 3, 3, LAT, CH), (27 * LAT) ** -0.5, 0.109375),
        "conv_bias": bell_draw(seeds[7], (CH,), 0.5, 3.0, (), jnp.float32),
        "res_weight": bell_draw(seeds[8], (3, 3, 3, CH, CH), (27 * CH) ** -0.5, 0.078125),
        "res_bias": bell_draw(seeds[9], (CH,), 0.5, 3.0, (), jnp.float32),
    }


def region_latent(rows, modulation, triple_weight, out_weight, gate, latent_weight):
    floats = rows.astype(jnp.float32)
    normed = floats * lax.rsqrt(lax.optimization_barrier(jnp.mean(floats * floats, axis=-1, keepdims=True)) + 1e-06)
    modulated = (normed * (1.0 + modulation[1]) + modulation[0]).astype(jnp.bfloat16)
    triples = jnp.dot(modulated, triple_weight.reshape(D, 3 * HEADS * HEAD_DIM), preferred_element_type=jnp.float32)
    triples = triples.astype(jnp.bfloat16).reshape(SEQ, 3, HEADS, HEAD_DIM).astype(jnp.float32)
    scores = jnp.einsum('qhd,khd->hqk', triples[:, 0], triples[:, 1]) * HEAD_DIM ** (-0.5)
    row_max = lax.optimization_barrier(jnp.max(scores, axis=-1, keepdims=True))
    weights = jnp.exp(scores - row_max)
    probs = (weights / lax.optimization_barrier(jnp.sum(weights, axis=-1, keepdims=True))).astype(jnp.bfloat16)
    attended = jnp.einsum('hqk,khd->qhd', probs.astype(jnp.float32), triples[:, 2])
    attended = attended.astype(jnp.bfloat16).reshape(SEQ, HEADS * HEAD_DIM)
    projected = jnp.dot(attended, out_weight, preferred_element_type=jnp.float32)
    branch = (gate * projected).astype(jnp.bfloat16)
    latent = jnp.dot(rows, latent_weight, preferred_element_type=jnp.float32) + jnp.dot(branch, latent_weight, preferred_element_type=jnp.float32)
    return latent.astype(jnp.bfloat16).reshape(FRAMES, HB, WW, LAT)

def conv_grid(field, weight):
    frames, rows, cols, _ = field.shape
    padded = jnp.pad(field, ((1, 1), (1, 1), (1, 1), (0, 0)))
    summed = jnp.zeros((frames * rows * cols, weight.shape[-1]), jnp.float32)
    for depth in range(3):
        for across in range(3):
            for along in range(3):
                view = padded[depth:depth + frames, across:across + rows, along:along + cols]
                summed = summed + jnp.dot(view.reshape(frames * rows * cols, -1), weight[depth, across, along], preferred_element_type=jnp.float32)
    return summed.reshape(frames, rows, cols, weight.shape[-1])

def reference(tokens, modulation, triple_weight, out_weight, gate, latent_weight, conv_weight, conv_bias, res_weight, res_bias):
    latents = lax.map(lambda rows: region_latent(rows, modulation, triple_weight, out_weight, gate, latent_weight), tokens)
    grid = jnp.transpose(latents, (1, 0, 2, 3, 4)).reshape(FRAMES, HH, WW, LAT)
    coarse = jax.nn.silu(conv_grid(grid, conv_weight) + conv_bias).astype(jnp.bfloat16)
    upscaled = jnp.repeat(jnp.repeat(coarse, 2, axis=1), 2, axis=2)
    result = jax.nn.silu(upscaled.astype(jnp.float32) + conv_grid(upscaled, res_weight) + res_bias)
    return result.astype(jnp.bfloat16)
```

```python
import math

import jax
import jax.numpy as jnp
from jax import lax
from jax.experimental import pallas as pl
from jax.experimental.pallas import tpu as pltpu
from jax.sharding import PartitionSpec as P

MESH = pl.DeviceIdType.MESH
F32 = jnp.float32
BF16 = jnp.bfloat16

D = 4096
HD = 128
FR = 16
BLK = 128
SUBS = 2
SUB = BLK // SUBS
LAT = 128
CH = 256
NZ = 8
W_CUT = 1408
EXP_SCALE = HD ** (-0.5) * math.log2(math.e)


def kernel(
    tok_ref, mod_ref, w_hbm, ow_hbm, gate_ref, lw_hbm, cw_hbm, cb_ref, rw_hbm, rb_ref,
    out_ref,
    xall, xown, wv, lw, ow, cw, rw, qs, kt, v2, radd, rmine, rbuf, mrecv, msend, mfull,
    lsend, lrecv, ext, coarse, cols2,
    local_sem, wloc_sem, swx_send, swx_recv, sww_send, sww_recv, swr_send, swr_recv,
    ring_send, ring_recv, sib_send, sib_recv, m_send, m_recv, mx_send, mx_recv,
    l_send, l_recv, h_send, h_recv,
):
    g = lax.axis_index("grp")
    t = lax.axis_index("tok")
    n_x = lax.axis_size("grp") // 4
    n_g = lax.axis_size("grp")
    core = lax.rem(g, 2)
    pair = g - core
    x = lax.rem(g // 2, n_x)
    y_hi = g // (2 * n_x)
    y_lo = t // NZ
    z = lax.rem(t, NZ)
    swapped = core != y_lo
    head = core * NZ + z
    mate_grp = pair + y_lo
    far_grp = (1 - y_hi) * (2 * n_x) + x * 2 + y_lo
    mate_tok = head
    sib_grp = pair + 1 - core
    up_tok = y_lo * NZ + lax.rem(z + 1, NZ)
    down_tok = y_lo * NZ + lax.rem(z + NZ - 1, NZ)
    outer = g + 2 * core - 1
    has_outer = jnp.logical_and(outer >= 0, outer < n_g)

    ext[...] = jnp.zeros_like(ext)

    barrier = pltpu.get_barrier_semaphore()

    def greet(grp, tok):
        pl.semaphore_signal(barrier, inc=1, device_id=(grp, tok), device_id_type=MESH)

    def greet_row(step, carry):
        other = lax.rem(t + step, FR)

        @pl.when(step > 0)
        def _():
            greet(g, other)

        greet(sib_grp, other)
        return carry

    lax.fori_loop(0, FR, greet_row, 0)
    for step in range(1, 4):
        greet(y_hi * (2 * n_x) + lax.rem(x + step, n_x) * 2 + core, t)

    @pl.when(swapped)
    def _():
        greet(far_grp, mate_tok)

    @pl.when(has_outer)
    def _():
        greet(outer, t)

        @pl.when(t > 0)
        def _():
            greet(outer, t - 1)

        @pl.when(t < FR - 1)
        def _():
            greet(outer, t + 1)

    guests = 2 * FR - 1 + 3 + jnp.where(swapped, 1, 0) + jnp.where(
        has_outer, 1 + jnp.where(t > 0, 1, 0) + jnp.where(t < FR - 1, 1, 0), 0
    )

    load_lw = pltpu.make_async_copy(lw_hbm, lw, local_sem.at[0])
    load_ow = pltpu.make_async_copy(ow_hbm.at[core, :, x], ow, local_sem.at[1])
    load_cw = pltpu.make_async_copy(cw_hbm, cw, local_sem.at[2])
    load_rw = pltpu.make_async_copy(rw_hbm, rw, local_sem.at[3])
    load_lw.start()
    load_ow.start()
    load_w = pltpu.make_async_copy(w_hbm, wv, wloc_sem.at[0])

    @pl.when(jnp.logical_not(swapped))
    def _():
        load_w.start()

    load_cw.start()
    load_rw.start()

    v2[:, HD:] = jnp.ones((v2.shape[0], HD), BF16)
    radd[...] = jnp.zeros_like(radd)

    def rows_of(sub):
        return pl.ds(sub * SUB, SUB)

    def swap_x(sub):
        return pltpu.make_async_remote_copy(
            src_ref=xown.at[rows_of(sub)],
            dst_ref=xall.at[t, rows_of(sub)],
            send_sem=swx_send.at[sub],
            recv_sem=swx_recv.at[sub],
            device_id=(mate_grp, mate_tok),
            device_id_type=MESH,
        )

    def wait_swap_x(sub):
        pltpu.make_async_copy(
            xall.at[head, rows_of(sub)], xall.at[head, rows_of(sub)], swx_recv.at[sub]
        ).wait()

    def swap_w(part):
        rows = pl.ds(0, W_CUT) if part == 0 else pl.ds(W_CUT, D - W_CUT)
        return pltpu.make_async_remote_copy(
            src_ref=w_hbm.at[rows],
            dst_ref=wv.at[rows],
            send_sem=sww_send.at[part],
            recv_sem=sww_recv.at[part],
            device_id=(mate_grp if part == 0 else far_grp, mate_tok),
            device_id_type=MESH,
        )

    def swap_r():
        return pltpu.make_async_remote_copy(
            src_ref=rmine,
            dst_ref=rbuf,
            send_sem=swr_send.at[0],
            recv_sem=swr_recv.at[0],
            device_id=(mate_grp, mate_tok),
            device_id_type=MESH,
        )

    def ring(way, step, sub):
        origin = lax.rem(z + (NZ - step if way == 0 else step), NZ)
        block = xall.at[core * NZ + origin, rows_of(sub)]
        return pltpu.make_async_remote_copy(
            src_ref=block,
            dst_ref=block,
            send_sem=ring_send.at[way, step, sub],
            recv_sem=ring_recv.at[way, step, sub],
            device_id=(g, up_tok if way == 0 else down_tok),
            device_id_type=MESH,
        )

    def wait_ring(way, step, sub):
        origin = lax.rem(z + (NZ - step if way == 0 else step), NZ)
        block = xall.at[core * NZ + origin, rows_of(sub)]
        pltpu.make_async_copy(block, block, ring_recv.at[way, step - 1, sub]).wait()

    def share(origin, sub):
        block = xall.at[core * NZ + origin, rows_of(sub)]
        return pltpu.make_async_remote_copy(
            src_ref=block,
            dst_ref=block,
            send_sem=sib_send.at[origin, sub],
            recv_sem=sib_recv.at[origin, sub],
            device_id=(sib_grp, t),
            device_id_type=MESH,
        )

    def origin_of(way, step):
        return lax.rem(z + (NZ - step if way == 0 else step), NZ)

    reach = (4 - core, 3 + core)

    load_lw.wait()

    new = lax.broadcasted_iota(jnp.int32, (BLK, BLK), 0)
    old = lax.broadcasted_iota(jnp.int32, (BLK, BLK), 1)
    source = (lax.rem(new // 2, 4)) * 32 + (new // 8) * 2 + lax.rem(new, 2)
    pick = jnp.where(old == source, 1.0, 0.0).astype(BF16)

    def prepare(sub):
        own = jnp.dot(
            pick[sub * SUB : (sub + 1) * SUB], tok_ref[...], preferred_element_type=F32
        )
        rmine[rows_of(sub), :] = jnp.dot(own.astype(BF16), lw[...], preferred_element_type=F32)
        scale = lax.rsqrt(jnp.mean(own * own, axis=-1, keepdims=True) + 1e-06)
        made = (own * scale * (1.0 + mod_ref[1:2, :]) + mod_ref[0:1, :]).astype(BF16)

        @pl.when(swapped)
        def _():
            xown[rows_of(sub), :] = made

        @pl.when(jnp.logical_not(swapped))
        def _():
            xall[head, rows_of(sub), :] = made

    prepare(0)
    pl.semaphore_wait(barrier, guests)

    @pl.when(swapped)
    def _():
        swap_x(0).start()
        swap_w(1).start()

    @pl.when(jnp.logical_not(swapped))
    def _():
        ring(0, 0, 0).start()
        ring(1, 0, 0).start()
        share(z, 0).start()

    prepare(1)

    @pl.when(swapped)
    def _():
        swap_x(1).start()
        swap_w(0).start()
        swap_r().start()
        wait_swap_x(0)
        ring(0, 0, 0).start()
        ring(1, 0, 0).start()
        share(z, 0).start()
        wait_swap_x(1)

    ring(0, 0, 1).start()
    ring(1, 0, 1).start()
    share(z, 1).start()

    load_ow.wait()
    scaled = (ow[...].astype(F32) * gate_ref[...]).astype(BF16).reshape(NZ * 32, 256)
    cols = pl.ds(pl.multiple_of(t * 256, 256), 256)
    part = jnp.dot(scaled, lw[cols, :], preferred_element_type=F32)
    msend[...] = part.astype(BF16).reshape(NZ, 32, LAT)

    def fold_copy(other):
        return pltpu.make_async_remote_copy(
            src_ref=msend.at[lax.rem(other, NZ)],
            dst_ref=mrecv.at[t],
            send_sem=m_send.at[other],
            recv_sem=m_recv.at[t],
            device_id=(g, other),
            device_id_type=MESH,
        )

    mrecv[t] = msend[z]

    def fold_send(step, carry):
        fold_copy(lax.rem(t + step, FR)).start()
        return carry

    lax.fori_loop(1, FR, fold_send, 0)

    def fold_wait(step, carry):
        other = lax.rem(t + step, FR)
        pltpu.make_async_copy(mrecv.at[other], mrecv.at[other], m_recv.at[other]).wait()
        return carry

    def fold_sent(step, carry):
        fold_copy(lax.rem(t + step, FR)).wait_send()
        return carry

    def fold_rows(which):
        return mfull.at[pl.ds(pl.multiple_of(which * 32, 32), 32)]

    def spread(step):
        return pltpu.make_async_remote_copy(
            src_ref=fold_rows(x),
            dst_ref=fold_rows(x),
            send_sem=mx_send.at[step],
            recv_sem=mx_recv.at[x],
            device_id=(y_hi * (2 * n_x) + lax.rem(x + step, n_x) * 2 + core, t),
            device_id_type=MESH,
        )

    def project(kind, origin):
        slot = kind * NZ + origin
        triple = jnp.dot(xall[slot], wv[...], preferred_element_type=F32)
        qs[pl.ds(slot, BLK, stride=FR), :] = triple[:, :HD]
        at = pl.ds(pl.multiple_of(slot * BLK, BLK), BLK)
        kt[:, at] = triple[:, HD : 2 * HD].T.astype(BF16)
        v2[at, :HD] = triple[:, 2 * HD :].astype(BF16)

    def project_sib(origin):
        for sub in range(SUBS):
            block = xall.at[(1 - core) * NZ + origin, rows_of(sub)]
            pltpu.make_async_copy(block, block, sib_recv.at[origin, sub]).wait()
        project(1 - core, origin)

    def forward(step):
        for sub in range(SUBS):
            for way in range(2):

                @pl.when(step <= reach[way])
                def _():
                    wait_ring(way, step, sub)

                    @pl.when(step < reach[way])
                    def _():
                        ring(way, step, sub).start()

                    share(origin_of(way, step), sub).start()

    def both(step, work):
        def go(way, carry):
            work(lax.rem(z + NZ + (2 * way - 1) * step, NZ))
            return carry

        lax.fori_loop(0, 2, go, 0)

    forward(1)

    @pl.when(jnp.logical_not(swapped))
    def _():
        load_w.wait()
        rbuf[...] = rmine[...]

    @pl.when(swapped)
    def _():
        pltpu.make_async_copy(wv.at[pl.ds(W_CUT, D - W_CUT)], wv.at[pl.ds(W_CUT, D - W_CUT)], sww_recv.at[1]).wait()
        pltpu.make_async_copy(wv.at[pl.ds(0, W_CUT)], wv.at[pl.ds(0, W_CUT)], sww_recv.at[0]).wait()
        pltpu.make_async_copy(rbuf, rbuf, swr_recv.at[0]).wait()

    def first(n, carry):
        project(core, lax.rem(z + NZ + lax.rem(n + 1, 3) - 1, NZ))
        return carry

    lax.fori_loop(0, 3, first, 0)
    project_sib(z)
    radd[pl.ds(head, BLK, stride=FR), :] = rbuf[...]
    lax.fori_loop(1, FR, fold_wait, 0)
    total = mrecv[0].astype(F32)
    for other in range(1, FR):
        total = total + mrecv[other].astype(F32)
    mfull[pl.ds(pl.multiple_of(x * 32, 32), 32), :] = total.astype(BF16)
    for step in range(1, 4):
        spread(step).start()

    forward(2)
    both(2, lambda origin: project(core, origin))
    both(1, project_sib)
    forward(3)
    both(3, lambda origin: project(core, origin))
    both(2, project_sib)
    both(3, project_sib)
    for step in range(1, 4):
        there = lax.rem(x + step, n_x)
        pltpu.make_async_copy(fold_rows(there), fold_rows(there), mx_recv.at[there]).wait()
    forward(4)
    last = lax.rem(z + 4, NZ)
    project(core, last)
    project_sib(last)

    home = pair + y_lo

    def latent_copy(target):
        return pltpu.make_async_remote_copy(
            src_ref=lsend.at[target],
            dst_ref=lrecv.at[head],
            send_sem=l_send.at[target],
            recv_sem=l_recv.at[head],
            device_id=(home, target),
            device_id_type=MESH,
        )

    def is_self(target):
        return jnp.logical_and(home == g, target == t)

    def attend(n, carry):
        two = lax.rem(n + t // 2 + 1, FR // 2)
        at = pl.ds(pl.multiple_of(two * 256, 256), 256)
        scores = jnp.dot(qs[at, :].astype(BF16), kt[...], preferred_element_type=F32)
        top = jnp.max(scores, axis=-1, keepdims=True)
        probs = jnp.exp2((scores - top) * EXP_SCALE).astype(BF16)
        summed = jnp.dot(probs, v2[...], preferred_element_type=F32)
        attended = (summed[:, :HD] / summed[:, HD:]).astype(BF16)
        latent = jnp.dot(attended, mfull[...], preferred_element_type=F32) + radd[at, :]
        pieces = latent.astype(BF16).reshape(2, BLK, LAT)
        lsend[pl.ds(pl.multiple_of(two * 2, 2), 2)] = pieces
        for half in range(2):
            target = two * 2 + half

            @pl.when(jnp.logical_not(is_self(target)))
            def _():
                latent_copy(target).start()

            @pl.when(is_self(target))
            def _():
                lrecv[head] = pieces[half]

        return carry

    lax.fori_loop(0, FR // 2, attend, 0)

    def latent_wait(n, carry):
        @pl.when(jnp.logical_not(jnp.logical_and(core == y_lo, n == head)))
        def _():
            pltpu.make_async_copy(lrecv.at[n], lrecv.at[n], l_recv.at[n]).wait()

        return carry

    lax.fori_loop(0, FR, latent_wait, 0)
    tile = lrecv[0].astype(F32)
    for n in range(1, FR):
        tile = tile + lrecv[n].astype(F32)
    ext[2:6, 2:4] = tile.astype(BF16).reshape(4, 2, FR, LAT)

    def halo(dg, dt):
        rows_src, rows_dst = {0: ((2, 4), (2, 4)), 1: ((4, 2), (0, 2)), -1: ((2, 2), (6, 2))}[dg]
        cols_dst = {0: 2, 1: 0, -1: 4}[dt]
        at = (dg + 1) * 3 + dt + 1
        return pltpu.make_async_remote_copy(
            src_ref=ext.at[pl.ds(*rows_src), pl.ds(2, 2)],
            dst_ref=ext.at[pl.ds(*rows_dst), pl.ds(cols_dst, 2)],
            send_sem=h_send.at[at],
            recv_sem=h_recv.at[at],
            device_id=(g + dg, t + dt),
            device_id_type=MESH,
        )

    def inside(dg, dt):
        ok = jnp.logical_and(g + dg >= 0, g + dg < n_g)
        return jnp.logical_and(ok, jnp.logical_and(t + dt >= 0, t + dt < FR))

    ways = [(dg, dt) for dg in (-1, 0, 1) for dt in (-1, 0, 1) if (dg, dt) != (0, 0)]
    for dg, dt in ways:

        @pl.when(inside(dg, dt))
        def _():
            halo(dg, dt).start()

    load_cw.wait()
    load_rw.wait()
    for dg, dt in ways:

        @pl.when(inside(-dg, -dt))
        def _():
            halo(dg, dt).wait_recv()

    def over_frames(three, rows):
        frame = lax.rem(lax.broadcasted_iota(jnp.int32, (rows, CH), 0), FR)
        before = pltpu.roll(three[0], 1, 0)
        after = pltpu.roll(three[2], rows - 1, 0)
        return (
            three[1]
            + jnp.where(frame > 0, before, 0.0)
            + jnp.where(frame < FR - 1, after, 0.0)
        )

    def silu(v):
        return v / (1.0 + jnp.exp(-v))

    views = [
        ext[b : b + 6, c : c + 4].reshape(24 * FR, LAT) for b in range(3) for c in range(3)
    ]
    cells = jnp.concatenate(views, axis=1)
    three = [jnp.dot(cells, cw[a], preferred_element_type=F32) for a in range(3)]
    made = silu(over_frames(three, 24 * FR) + cb_ref[...]).astype(BF16)
    coarse[...] = made.reshape(6, 4, FR, CH)

    @pl.when(g == 0)
    def _():
        coarse[0:1] = jnp.zeros((1, 4, FR, CH), BF16)

    @pl.when(g == n_g - 1)
    def _():
        coarse[5:6] = jnp.zeros((1, 4, FR, CH), BF16)

    @pl.when(t == 0)
    def _():
        coarse[:, 0:1] = jnp.zeros((6, 1, FR, CH), BF16)

    @pl.when(t == FR - 1)
    def _():
        coarse[:, 3:4] = jnp.zeros((6, 1, FR, CH), BF16)

    rows = 8 * FR
    for p in range(2):
        for q in range(2):
            for b in range(3):
                for c in range(3):
                    r0 = 1 + (p + b - 1) // 2
                    c0 = 1 + (q + c - 1) // 2
                    at = (p * 2 + q) * rows
                    k = (b * 3 + c) * CH
                    cols2[at : at + rows, k : k + CH] = coarse[
                        r0 : r0 + 4, c0 : c0 + 2
                    ].reshape(rows, CH)
    three = [jnp.dot(cols2[...], rw[a], preferred_element_type=F32) for a in range(3)]
    mixed = over_frames(three, 4 * rows)
    center = coarse[1:5, 1:3].reshape(rows, CH).astype(F32)
    for n in range(4):
        result = silu(center + mixed[n * rows : (n + 1) * rows] + rb_ref[...])
        out_ref[n] = result.astype(BF16).reshape(4, 2, FR, CH)

    for sub in range(SUBS):

        @pl.when(swapped)
        def _():
            swap_x(sub).wait_send()

        for way in range(2):
            for step in range(4):

                @pl.when(step < reach[way])
                def _():
                    ring(way, step, sub).wait_send()

        for origin in range(NZ):
            share(origin, sub).wait_send()

    @pl.when(swapped)
    def _():
        swap_w(0).wait_send()
        swap_w(1).wait_send()
        swap_r().wait_send()

    lax.fori_loop(1, FR, fold_sent, 0)
    for step in range(1, 4):
        spread(step).wait_send()

    def latent_sent(target, carry):
        @pl.when(jnp.logical_not(is_self(target)))
        def _():
            latent_copy(target).wait_send()

        return carry

    lax.fori_loop(0, FR, latent_sent, 0)
    for dg, dt in ways:

        @pl.when(inside(dg, dt))
        def _():
            halo(dg, dt).wait_send()


def shards(
    tokens,
    modulation,
    triple_weight,
    out_weight,
    gate,
    latent_weight,
    conv_weight,
    conv_bias,
    res_weight,
    res_bias,
):
    vmem = pl.BlockSpec(memory_space=pltpu.VMEM)
    hbm = pl.BlockSpec(memory_space=pl.ANY)
    dma = pltpu.SemaphoreType.DMA
    out = pl.pallas_call(
        kernel,
        out_shape=jax.ShapeDtypeStruct((4, 4, 2, FR, CH), BF16),
        in_specs=[vmem, vmem, hbm, hbm, vmem, hbm, hbm, vmem, hbm, vmem],
        out_specs=vmem,
        scratch_shapes=[
            pltpu.VMEM((FR, BLK, D), BF16),
            pltpu.VMEM((BLK, D), BF16),
            pltpu.VMEM((D, 3 * HD), BF16),
            pltpu.VMEM((D, LAT), BF16),
            pltpu.VMEM((NZ, 32, 256), BF16),
            pltpu.VMEM((3, 9 * LAT, CH), BF16),
            pltpu.VMEM((3, 9 * CH, CH), BF16),
            pltpu.VMEM((FR * BLK, HD), F32),
            pltpu.VMEM((HD, FR * BLK), BF16),
            pltpu.VMEM((FR * BLK, 2 * HD), BF16),
            pltpu.VMEM((FR * BLK, LAT), F32),
            pltpu.VMEM((BLK, LAT), F32),
            pltpu.VMEM((BLK, LAT), F32),
            pltpu.VMEM((FR, 32, LAT), BF16),
            pltpu.VMEM((NZ, 32, LAT), BF16),
            pltpu.VMEM((HD, LAT), BF16),
            pltpu.VMEM((FR, BLK, LAT), BF16),
            pltpu.VMEM((FR, BLK, LAT), BF16),
            pltpu.VMEM((8, 6, FR, LAT), BF16),
            pltpu.VMEM((6, 4, FR, CH), BF16),
            pltpu.VMEM((4 * 8 * FR, 9 * CH), BF16),
            dma((4,)),
            dma((1,)),
            dma((SUBS,)), dma((SUBS,)),
            dma((2,)), dma((2,)),
            dma((1,)), dma((1,)),
            dma((2, 4, SUBS)), dma((2, 4, SUBS)),
            dma((NZ, SUBS)), dma((NZ, SUBS)),
            dma((FR,)), dma((FR,)),
            dma((4,)), dma((4,)),
            dma((FR,)), dma((FR,)),
            dma((9,)), dma((9,)),
        ],
        compiler_params=pltpu.CompilerParams(
            collective_id=0, has_side_effects=True, vmem_limit_bytes=60 * 2**20
        ),
        cost_estimate=pl.CostEstimate(
            flops=13 * 10**9, bytes_accessed=14 * 10**6, transcendentals=5 * 10**6
        ),
    )(
        tokens[0],
        modulation,
        triple_weight.reshape(D, 3 * HD),
        out_weight.reshape(2, NZ, 4, 32, 256),
        gate.reshape(1, 256),
        latent_weight,
        conv_weight.reshape(3, 9 * LAT, CH),
        conv_bias.reshape(1, CH),
        res_weight.reshape(3, 9 * CH, CH),
        res_bias.reshape(1, CH),
    )
    out = out.reshape(2, 2, 4, 2, FR, CH)
    return out.transpose(4, 2, 0, 3, 1, 5).reshape(FR, 8, 4, CH)


def solution(mesh):
    placed = (
        P("grp", "tok", None),
        P(),
        P(None, None, "tok"),
        P(None, "tok"),
        P("tok"),
        P(),
        P(),
        P(),
        P(),
        P(),
    )
    return jax.shard_map(
        shards, mesh=mesh, in_specs=placed, out_specs=P(None, "grp", "tok", None), check_vma=False
    )
```

```python
import math

import jax
import jax.numpy as jnp
from jax import lax
from jax.experimental import pallas as pl
from jax.experimental.pallas import tpu as pltpu
from jax.sharding import PartitionSpec as P

MESH = pl.DeviceIdType.MESH
F32 = jnp.float32
BF16 = jnp.bfloat16

D = 4096
HD = 128
FR = 16
BLK = 128
SUBS = 2
SUB = BLK // SUBS
LAT = 128
CH = 256
NZ = 8
EXP_SCALE = HD ** (-0.5) * math.log2(math.e)


def kernel(
    tok_ref, mod_ref, w_hbm, ow_hbm, gate_ref, lw_hbm, cw_hbm, cb_ref, rw_hbm, rb_ref,
    out_ref,
    xall, xown, wv, lw, ow, cw, rw, qs, kt, v2, radd, rmine, rbuf, mrecv, msend, mfull,
    lsend, lrecv, ext, coarse, cols2,
    local_sem, wloc_sem, swx_send, swx_recv, sww_send, sww_recv, swr_send, swr_recv,
    ring_send, ring_recv, sib_send, sib_recv, m_send, m_recv, mx_send, mx_recv,
    l_send, l_recv, h_send, h_recv,
):
    g = lax.axis_index("grp")
    t = lax.axis_index("tok")
    n_x = lax.axis_size("grp") // 4
    n_g = lax.axis_size("grp")
    core = lax.rem(g, 2)
    pair = g - core
    x = lax.rem(g // 2, n_x)
    y_hi = g // (2 * n_x)
    y_lo = t // NZ
    z = lax.rem(t, NZ)
    swapped = core != y_lo
    head = core * NZ + z
    mate_grp = pair + y_lo
    far_grp = (1 - y_hi) * (2 * n_x) + x * 2 + y_lo
    mate_tok = head
    sib_grp = pair + 1 - core
    up_tok = y_lo * NZ + lax.rem(z + 1, NZ)
    down_tok = y_lo * NZ + lax.rem(z + NZ - 1, NZ)
    outer = g + 2 * core - 1
    has_outer = jnp.logical_and(outer >= 0, outer < n_g)

    ext[...] = jnp.zeros_like(ext)

    barrier = pltpu.get_barrier_semaphore()

    def greet(grp, tok):
        pl.semaphore_signal(barrier, inc=1, device_id=(grp, tok), device_id_type=MESH)

    def greet_row(step, carry):
        other = lax.rem(t + step, FR)

        @pl.when(step > 0)
        def _():
            greet(g, other)

        greet(sib_grp, other)
        return carry

    lax.fori_loop(0, FR, greet_row, 0)
    for step in range(1, 4):
        greet(y_hi * (2 * n_x) + lax.rem(x + step, n_x) * 2 + core, t)

    @pl.when(swapped)
    def _():
        greet(far_grp, mate_tok)

    @pl.when(has_outer)
    def _():
        greet(outer, t)

        @pl.when(t > 0)
        def _():
            greet(outer, t - 1)

        @pl.when(t < FR - 1)
        def _():
            greet(outer, t + 1)

    guests = 2 * FR - 1 + 3 + jnp.where(swapped, 1, 0) + jnp.where(
        has_outer, 1 + jnp.where(t > 0, 1, 0) + jnp.where(t < FR - 1, 1, 0), 0
    )

    load_lw = pltpu.make_async_copy(lw_hbm, lw, local_sem.at[0])
    load_ow = pltpu.make_async_copy(ow_hbm.at[core, :, x], ow, local_sem.at[1])
    load_cw = pltpu.make_async_copy(cw_hbm, cw, local_sem.at[2])
    load_rw = pltpu.make_async_copy(rw_hbm, rw, local_sem.at[3])
    load_lw.start()
    load_ow.start()

    def third(k):
        return wv.at[:, pl.ds(k * HD, HD)]

    def load_w(k):
        return pltpu.make_async_copy(w_hbm.at[k], third(k), wloc_sem.at[k])

    @pl.when(jnp.logical_not(swapped))
    def _():
        for k in range(3):
            load_w(k).start()

    load_cw.start()
    load_rw.start()

    v2[:, HD:] = jnp.ones((v2.shape[0], HD), BF16)
    radd[...] = jnp.zeros_like(radd)

    def rows_of(sub):
        return pl.ds(sub * SUB, SUB)

    def swap_x(sub):
        return pltpu.make_async_remote_copy(
            src_ref=xown.at[rows_of(sub)],
            dst_ref=xall.at[t, rows_of(sub)],
            send_sem=swx_send.at[sub],
            recv_sem=swx_recv.at[sub],
            device_id=(mate_grp, mate_tok),
            device_id_type=MESH,
        )

    def wait_swap_x(sub):
        pltpu.make_async_copy(
            xall.at[head, rows_of(sub)], xall.at[head, rows_of(sub)], swx_recv.at[sub]
        ).wait()

    def swap_w(k):
        return pltpu.make_async_remote_copy(
            src_ref=w_hbm.at[k],
            dst_ref=third(k),
            send_sem=sww_send.at[k],
            recv_sem=sww_recv.at[k],
            device_id=(mate_grp if k == 2 else far_grp, mate_tok),
            device_id_type=MESH,
        )

    def swap_r():
        return pltpu.make_async_remote_copy(
            src_ref=rmine,
            dst_ref=rbuf,
            send_sem=swr_send.at[0],
            recv_sem=swr_recv.at[0],
            device_id=(mate_grp, mate_tok),
            device_id_type=MESH,
        )

    def ring(way, step, sub):
        origin = lax.rem(z + (NZ - step if way == 0 else step), NZ)
        block = xall.at[core * NZ + origin, rows_of(sub)]
        return pltpu.make_async_remote_copy(
            src_ref=block,
            dst_ref=block,
            send_sem=ring_send.at[way, step, sub],
            recv_sem=ring_recv.at[way, step, sub],
            device_id=(g, up_tok if way == 0 else down_tok),
            device_id_type=MESH,
        )

    def wait_ring(way, step, sub):
        origin = lax.rem(z + (NZ - step if way == 0 else step), NZ)
        block = xall.at[core * NZ + origin, rows_of(sub)]
        pltpu.make_async_copy(block, block, ring_recv.at[way, step - 1, sub]).wait()

    def share(origin, sub):
        block = xall.at[core * NZ + origin, rows_of(sub)]
        return pltpu.make_async_remote_copy(
            src_ref=block,
            dst_ref=block,
            send_sem=sib_send.at[origin, sub],
            recv_sem=sib_recv.at[origin, sub],
            device_id=(sib_grp, t),
            device_id_type=MESH,
        )

    def origin_of(way, step):
        return lax.rem(z + (NZ - step if way == 0 else step), NZ)

    reach = (4 - core, 3 + core)

    load_lw.wait()

    new = lax.broadcasted_iota(jnp.int32, (BLK, BLK), 0)
    old = lax.broadcasted_iota(jnp.int32, (BLK, BLK), 1)
    source = (lax.rem(new // 2, 4)) * 32 + (new // 8) * 2 + lax.rem(new, 2)
    pick = jnp.where(old == source, 1.0, 0.0).astype(BF16)

    def prepare(sub):
        own = jnp.dot(
            pick[sub * SUB : (sub + 1) * SUB], tok_ref[...], preferred_element_type=F32
        )
        rmine[rows_of(sub), :] = jnp.dot(own.astype(BF16), lw[...], preferred_element_type=F32)
        scale = lax.rsqrt(jnp.mean(own * own, axis=-1, keepdims=True) + 1e-06)
        made = (own * scale * (1.0 + mod_ref[1:2, :]) + mod_ref[0:1, :]).astype(BF16)

        @pl.when(swapped)
        def _():
            xown[rows_of(sub), :] = made

        @pl.when(jnp.logical_not(swapped))
        def _():
            xall[head, rows_of(sub), :] = made

    prepare(0)
    pl.semaphore_wait(barrier, guests)

    @pl.when(swapped)
    def _():
        swap_x(0).start()
        swap_w(0).start()
        swap_w(1).start()

    @pl.when(jnp.logical_not(swapped))
    def _():
        ring(0, 0, 0).start()
        ring(1, 0, 0).start()
        share(z, 0).start()

    prepare(1)

    @pl.when(swapped)
    def _():
        swap_x(1).start()
        swap_w(2).start()
        swap_r().start()
        wait_swap_x(0)
        ring(0, 0, 0).start()
        ring(1, 0, 0).start()
        share(z, 0).start()
        wait_swap_x(1)

    ring(0, 0, 1).start()
    ring(1, 0, 1).start()
    share(z, 1).start()

    load_ow.wait()
    scaled = (ow[...].astype(F32) * gate_ref[...]).astype(BF16).reshape(NZ * 32, 256)
    cols = pl.ds(pl.multiple_of(t * 256, 256), 256)
    part = jnp.dot(scaled, lw[cols, :], preferred_element_type=F32)
    msend[...] = part.astype(BF16).reshape(NZ, 32, LAT)

    def fold_copy(other):
        return pltpu.make_async_remote_copy(
            src_ref=msend.at[lax.rem(other, NZ)],
            dst_ref=mrecv.at[t],
            send_sem=m_send.at[other],
            recv_sem=m_recv.at[t],
            device_id=(g, other),
            device_id_type=MESH,
        )

    mrecv[t] = msend[z]

    def fold_send(step, carry):
        fold_copy(lax.rem(t + step, FR)).start()
        return carry

    lax.fori_loop(1, FR, fold_send, 0)

    def fold_wait(step, carry):
        other = lax.rem(t + step, FR)
        pltpu.make_async_copy(mrecv.at[other], mrecv.at[other], m_recv.at[other]).wait()
        return carry

    def fold_sent(step, carry):
        fold_copy(lax.rem(t + step, FR)).wait_send()
        return carry

    def fold_rows(which):
        return mfull.at[pl.ds(pl.multiple_of(which * 32, 32), 32)]

    def spread(step):
        return pltpu.make_async_remote_copy(
            src_ref=fold_rows(x),
            dst_ref=fold_rows(x),
            send_sem=mx_send.at[step],
            recv_sem=mx_recv.at[x],
            device_id=(y_hi * (2 * n_x) + lax.rem(x + step, n_x) * 2 + core, t),
            device_id_type=MESH,
        )

    def project(kind, origin):
        slot = kind * NZ + origin
        triple = jnp.dot(xall[slot], wv[...], preferred_element_type=F32)
        qs[pl.ds(slot, BLK, stride=FR), :] = triple[:, :HD]
        at = pl.ds(pl.multiple_of(slot * BLK, BLK), BLK)
        kt[:, at] = triple[:, HD : 2 * HD].T.astype(BF16)
        v2[at, :HD] = triple[:, 2 * HD :].astype(BF16)

    def project_sib(origin):
        for sub in range(SUBS):
            block = xall.at[(1 - core) * NZ + origin, rows_of(sub)]
            pltpu.make_async_copy(block, block, sib_recv.at[origin, sub]).wait()
        project(1 - core, origin)

    def forward(step):
        for sub in range(SUBS):
            for way in range(2):

                @pl.when(step <= reach[way])
                def _():
                    wait_ring(way, step, sub)

                    @pl.when(step < reach[way])
                    def _():
                        ring(way, step, sub).start()

                    share(origin_of(way, step), sub).start()

    def both(step, work):
        def go(way, carry):
            work(lax.rem(z + NZ + (2 * way - 1) * step, NZ))
            return carry

        lax.fori_loop(0, 2, go, 0)

    forward(1)

    @pl.when(jnp.logical_not(swapped))
    def _():
        for k in range(3):
            load_w(k).wait()
        rbuf[...] = rmine[...]

    @pl.when(swapped)
    def _():
        for k in range(3):
            swap_w(k).wait_recv()
        pltpu.make_async_copy(rbuf, rbuf, swr_recv.at[0]).wait()

    def first(n, carry):
        project(core, lax.rem(z + NZ + lax.rem(n + 1, 3) - 1, NZ))
        return carry

    lax.fori_loop(0, 3, first, 0)
    project_sib(z)
    radd[pl.ds(head, BLK, stride=FR), :] = rbuf[...]
    lax.fori_loop(1, FR, fold_wait, 0)
    total = mrecv[0].astype(F32)
    for other in range(1, FR):
        total = total + mrecv[other].astype(F32)
    mfull[pl.ds(pl.multiple_of(x * 32, 32), 32), :] = total.astype(BF16)
    for step in range(1, 4):
        spread(step).start()

    forward(2)
    both(2, lambda origin: project(core, origin))
    both(1, project_sib)
    forward(3)
    both(3, lambda origin: project(core, origin))
    both(2, project_sib)
    both(3, project_sib)
    for step in range(1, 4):
        there = lax.rem(x + step, n_x)
        pltpu.make_async_copy(fold_rows(there), fold_rows(there), mx_recv.at[there]).wait()
    forward(4)
    last = lax.rem(z + 4, NZ)
    project(core, last)
    project_sib(last)

    home = pair + y_lo

    def latent_copy(target):
        return pltpu.make_async_remote_copy(
            src_ref=lsend.at[target],
            dst_ref=lrecv.at[head],
            send_sem=l_send.at[target],
            recv_sem=l_recv.at[head],
            device_id=(home, target),
            device_id_type=MESH,
        )

    def is_self(target):
        return jnp.logical_and(home == g, target == t)

    def attend(n, carry):
        two = lax.rem(n + t // 2 + 1, FR // 2)
        at = pl.ds(pl.multiple_of(two * 256, 256), 256)
        scores = jnp.dot(qs[at, :].astype(BF16), kt[...], preferred_element_type=F32)
        top = jnp.max(scores, axis=-1, keepdims=True)
        probs = jnp.exp2((scores - top) * EXP_SCALE).astype(BF16)
        summed = jnp.dot(probs, v2[...], preferred_element_type=F32)
        attended = (summed[:, :HD] / summed[:, HD:]).astype(BF16)
        latent = jnp.dot(attended, mfull[...], preferred_element_type=F32) + radd[at, :]
        pieces = latent.astype(BF16).reshape(2, BLK, LAT)
        lsend[pl.ds(pl.multiple_of(two * 2, 2), 2)] = pieces
        for half in range(2):
            target = two * 2 + half

            @pl.when(jnp.logical_not(is_self(target)))
            def _():
                latent_copy(target).start()

            @pl.when(is_self(target))
            def _():
                lrecv[head] = pieces[half]

        return carry

    lax.fori_loop(0, FR // 2, attend, 0)

    def latent_wait(n, carry):
        @pl.when(jnp.logical_not(jnp.logical_and(core == y_lo, n == head)))
        def _():
            pltpu.make_async_copy(lrecv.at[n], lrecv.at[n], l_recv.at[n]).wait()

        return carry

    lax.fori_loop(0, FR, latent_wait, 0)
    tile = lrecv[0].astype(F32)
    for n in range(1, FR):
        tile = tile + lrecv[n].astype(F32)
    ext[2:6, 2:4] = tile.astype(BF16).reshape(4, 2, FR, LAT)

    def halo(dg, dt):
        rows_src, rows_dst = {0: ((2, 4), (2, 4)), 1: ((4, 2), (0, 2)), -1: ((2, 2), (6, 2))}[dg]
        cols_dst = {0: 2, 1: 0, -1: 4}[dt]
        at = (dg + 1) * 3 + dt + 1
        return pltpu.make_async_remote_copy(
            src_ref=ext.at[pl.ds(*rows_src), pl.ds(2, 2)],
            dst_ref=ext.at[pl.ds(*rows_dst), pl.ds(cols_dst, 2)],
            send_sem=h_send.at[at],
            recv_sem=h_recv.at[at],
            device_id=(g + dg, t + dt),
            device_id_type=MESH,
        )

    def inside(dg, dt):
        ok = jnp.logical_and(g + dg >= 0, g + dg < n_g)
        return jnp.logical_and(ok, jnp.logical_and(t + dt >= 0, t + dt < FR))

    ways = [(dg, dt) for dg in (-1, 0, 1) for dt in (-1, 0, 1) if (dg, dt) != (0, 0)]
    for dg, dt in ways:

        @pl.when(inside(dg, dt))
        def _():
            halo(dg, dt).start()

    load_cw.wait()
    load_rw.wait()
    for dg, dt in ways:

        @pl.when(inside(-dg, -dt))
        def _():
            halo(dg, dt).wait_recv()

    def over_frames(three, rows):
        frame = lax.rem(lax.broadcasted_iota(jnp.int32, (rows, CH), 0), FR)
        before = pltpu.roll(three[0], 1, 0)
        after = pltpu.roll(three[2], rows - 1, 0)
        return (
            three[1]
            + jnp.where(frame > 0, before, 0.0)
            + jnp.where(frame < FR - 1, after, 0.0)
        )

    def silu(v):
        return v / (1.0 + jnp.exp(-v))

    views = [
        ext[b : b + 6, c : c + 4].reshape(24 * FR, LAT) for b in range(3) for c in range(3)
    ]
    cells = jnp.concatenate(views, axis=1)
    three = [jnp.dot(cells, cw[a], preferred_element_type=F32) for a in range(3)]
    made = silu(over_frames(three, 24 * FR) + cb_ref[...]).astype(BF16)
    coarse[...] = made.reshape(6, 4, FR, CH)

    @pl.when(g == 0)
    def _():
        coarse[0:1] = jnp.zeros((1, 4, FR, CH), BF16)

    @pl.when(g == n_g - 1)
    def _():
        coarse[5:6] = jnp.zeros((1, 4, FR, CH), BF16)

    @pl.when(t == 0)
    def _():
        coarse[:, 0:1] = jnp.zeros((6, 1, FR, CH), BF16)

    @pl.when(t == FR - 1)
    def _():
        coarse[:, 3:4] = jnp.zeros((6, 1, FR, CH), BF16)

    rows = 8 * FR
    for p in range(2):
        for q in range(2):
            for b in range(3):
                for c in range(3):
                    r0 = 1 + (p + b - 1) // 2
                    c0 = 1 + (q + c - 1) // 2
                    at = (p * 2 + q) * rows
                    k = (b * 3 + c) * CH
                    cols2[at : at + rows, k : k + CH] = coarse[
                        r0 : r0 + 4, c0 : c0 + 2
                    ].reshape(rows, CH)
    three = [jnp.dot(cols2[...], rw[a], preferred_element_type=F32) for a in range(3)]
    mixed = over_frames(three, 4 * rows)
    center = coarse[1:5, 1:3].reshape(rows, CH).astype(F32)
    for n in range(4):
        result = silu(center + mixed[n * rows : (n + 1) * rows] + rb_ref[...])
        out_ref[n] = result.astype(BF16).reshape(4, 2, FR, CH)

    for sub in range(SUBS):

        @pl.when(swapped)
        def _():
            swap_x(sub).wait_send()

        for way in range(2):
            for step in range(4):

                @pl.when(step < reach[way])
                def _():
                    ring(way, step, sub).wait_send()

        for origin in range(NZ):
            share(origin, sub).wait_send()

    @pl.when(swapped)
    def _():
        for k in range(3):
            swap_w(k).wait_send()
        swap_r().wait_send()

    lax.fori_loop(1, FR, fold_sent, 0)
    for step in range(1, 4):
        spread(step).wait_send()

    def latent_sent(target, carry):
        @pl.when(jnp.logical_not(is_self(target)))
        def _():
            latent_copy(target).wait_send()

        return carry

    lax.fori_loop(0, FR, latent_sent, 0)
    for dg, dt in ways:

        @pl.when(inside(dg, dt))
        def _():
            halo(dg, dt).wait_send()


def shards(
    tokens,
    modulation,
    triple_weight,
    out_weight,
    gate,
    latent_weight,
    conv_weight,
    conv_bias,
    res_weight,
    res_bias,
):
    vmem = pl.BlockSpec(memory_space=pltpu.VMEM)
    hbm = pl.BlockSpec(memory_space=pl.ANY)
    dma = pltpu.SemaphoreType.DMA
    out = pl.pallas_call(
        kernel,
        out_shape=jax.ShapeDtypeStruct((4, 4, 2, FR, CH), BF16),
        in_specs=[vmem, vmem, hbm, hbm, vmem, hbm, hbm, vmem, hbm, vmem],
        out_specs=vmem,
        scratch_shapes=[
            pltpu.VMEM((FR, BLK, D), BF16),
            pltpu.VMEM((BLK, D), BF16),
            pltpu.VMEM((D, 3 * HD), BF16),
            pltpu.VMEM((D, LAT), BF16),
            pltpu.VMEM((NZ, 32, 256), BF16),
            pltpu.VMEM((3, 9 * LAT, CH), BF16),
            pltpu.VMEM((3, 9 * CH, CH), BF16),
            pltpu.VMEM((FR * BLK, HD), F32),
            pltpu.VMEM((HD, FR * BLK), BF16),
            pltpu.VMEM((FR * BLK, 2 * HD), BF16),
            pltpu.VMEM((FR * BLK, LAT), F32),
            pltpu.VMEM((BLK, LAT), F32),
            pltpu.VMEM((BLK, LAT), F32),
            pltpu.VMEM((FR, 32, LAT), BF16),
            pltpu.VMEM((NZ, 32, LAT), BF16),
            pltpu.VMEM((HD, LAT), BF16),
            pltpu.VMEM((FR, BLK, LAT), BF16),
            pltpu.VMEM((FR, BLK, LAT), BF16),
            pltpu.VMEM((8, 6, FR, LAT), BF16),
            pltpu.VMEM((6, 4, FR, CH), BF16),
            pltpu.VMEM((4 * 8 * FR, 9 * CH), BF16),
            dma((4,)),
            dma((3,)),
            dma((SUBS,)), dma((SUBS,)),
            dma((3,)), dma((3,)),
            dma((1,)), dma((1,)),
            dma((2, 4, SUBS)), dma((2, 4, SUBS)),
            dma((NZ, SUBS)), dma((NZ, SUBS)),
            dma((FR,)), dma((FR,)),
            dma((4,)), dma((4,)),
            dma((FR,)), dma((FR,)),
            dma((9,)), dma((9,)),
        ],
        compiler_params=pltpu.CompilerParams(
            collective_id=0, has_side_effects=True, vmem_limit_bytes=60 * 2**20
        ),
        cost_estimate=pl.CostEstimate(
            flops=13 * 10**9, bytes_accessed=14 * 10**6, transcendentals=5 * 10**6
        ),
    )(
        tokens[0],
        modulation,
        triple_weight.transpose(1, 0, 2),
        out_weight.reshape(2, NZ, 4, 32, 256),
        gate.reshape(1, 256),
        latent_weight,
        conv_weight.reshape(3, 9 * LAT, CH),
        conv_bias.reshape(1, CH),
        res_weight.reshape(3, 9 * CH, CH),
        res_bias.reshape(1, CH),
    )
    out = out.reshape(2, 2, 4, 2, FR, CH)
    return out.transpose(4, 2, 0, 3, 1, 5).reshape(FR, 8, 4, CH)


def solution(mesh):
    placed = (
        P("grp", "tok", None),
        P(),
        P(None, None, "tok"),
        P(None, "tok"),
        P("tok"),
        P(),
        P(),
        P(),
        P(),
        P(),
    )
    return jax.shard_map(
        shards, mesh=mesh, in_specs=placed, out_specs=P(None, "grp", "tok", None), check_vma=False
    )
```

```python
import math

import jax
import jax.numpy as jnp
from jax import lax
from jax.experimental import pallas as pl
from jax.experimental.pallas import tpu as pltpu
from jax.sharding import PartitionSpec as P

MESH = pl.DeviceIdType.MESH
F32 = jnp.float32
BF16 = jnp.bfloat16

D = 4096
HD = 128
FR = 16
BLK = 128
SUBS = 4
SUB = BLK // SUBS
LAT = 128
CH = 256
NZ = 8
EARLY = 14 * BLK
EXP_SCALE = HD ** (-0.5) * math.log2(math.e)


def kernel(
    tok_ref, mod_ref, w_hbm, ow_hbm, gate_ref, lw_hbm, cw_hbm, cb_ref, rw_hbm, rb_ref,
    out_ref,
    xall, xown, wv, lw, ow, cw, rw, qs, kt, v2, radd, rmine, rbuf, mrecv, msend, mfull,
    lsend, lrecv, psend, precv, pmine, tops, sums, weights, order, ext, coarse, cols2,
    local_sem, wloc_sem, swx_send, swx_recv, sww_send, sww_recv, swr_send, swr_recv,
    ring_send, ring_recv, sib_send, sib_recv, m_send, m_recv, mx_send, mx_recv,
    l_send, l_recv, p_send, p_recv, h_send, h_recv,
):
    g = lax.axis_index("grp")
    t = lax.axis_index("tok")
    n_x = lax.axis_size("grp") // 4
    n_g = lax.axis_size("grp")
    core = lax.rem(g, 2)
    pair = g - core
    x = lax.rem(g // 2, n_x)
    y_hi = g // (2 * n_x)
    y_lo = t // NZ
    z = lax.rem(t, NZ)
    swapped = core != y_lo
    head = core * NZ + z
    mate_grp = pair + y_lo
    far_grp = (1 - y_hi) * (2 * n_x) + x * 2 + y_lo
    mate_tok = head
    sib_grp = pair + 1 - core
    up_tok = y_lo * NZ + lax.rem(z + 1, NZ)
    down_tok = y_lo * NZ + lax.rem(z + NZ - 1, NZ)
    outer = g + 2 * core - 1
    has_outer = jnp.logical_and(outer >= 0, outer < n_g)

    ext[...] = jnp.zeros_like(ext)

    barrier = pltpu.get_barrier_semaphore()

    def greet(grp, tok):
        pl.semaphore_signal(barrier, inc=1, device_id=(grp, tok), device_id_type=MESH)

    def greet_row(step, carry):
        other = lax.rem(t + step, FR)

        @pl.when(step > 0)
        def _():
            greet(g, other)

        greet(sib_grp, other)
        return carry

    lax.fori_loop(0, FR, greet_row, 0)
    for step in range(1, 4):
        greet(y_hi * (2 * n_x) + lax.rem(x + step, n_x) * 2 + core, t)

    @pl.when(swapped)
    def _():
        greet(far_grp, mate_tok)

    @pl.when(has_outer)
    def _():
        greet(outer, t)

        @pl.when(t > 0)
        def _():
            greet(outer, t - 1)

        @pl.when(t < FR - 1)
        def _():
            greet(outer, t + 1)

    guests = 2 * FR - 1 + 3 + jnp.where(swapped, 1, 0) + jnp.where(
        has_outer, 1 + jnp.where(t > 0, 1, 0) + jnp.where(t < FR - 1, 1, 0), 0
    )

    load_lw = pltpu.make_async_copy(lw_hbm, lw, local_sem.at[0])
    load_ow = pltpu.make_async_copy(ow_hbm.at[core, :, x], ow, local_sem.at[1])
    load_cw = pltpu.make_async_copy(cw_hbm, cw, local_sem.at[2])
    load_rw = pltpu.make_async_copy(rw_hbm, rw, local_sem.at[3])
    load_lw.start()
    load_ow.start()

    def third(k):
        return wv.at[:, pl.ds(k * HD, HD)]

    def load_w(k):
        return pltpu.make_async_copy(w_hbm.at[k], third(k), wloc_sem.at[k])

    @pl.when(jnp.logical_not(swapped))
    def _():
        for k in range(3):
            load_w(k).start()

    load_cw.start()
    load_rw.start()

    def rows_of(sub):
        return pl.ds(sub * SUB, SUB)

    def swap_x(sub):
        return pltpu.make_async_remote_copy(
            src_ref=xown.at[rows_of(sub)],
            dst_ref=xall.at[t, rows_of(sub)],
            send_sem=swx_send.at[sub],
            recv_sem=swx_recv.at[sub],
            device_id=(mate_grp, mate_tok),
            device_id_type=MESH,
        )

    def wait_swap_x(sub):
        pltpu.make_async_copy(
            xall.at[head, rows_of(sub)], xall.at[head, rows_of(sub)], swx_recv.at[sub]
        ).wait()

    def swap_w(k):
        return pltpu.make_async_remote_copy(
            src_ref=w_hbm.at[k],
            dst_ref=third(k),
            send_sem=sww_send.at[k],
            recv_sem=sww_recv.at[k],
            device_id=(mate_grp if k == 2 else far_grp, mate_tok),
            device_id_type=MESH,
        )

    def swap_r():
        return pltpu.make_async_remote_copy(
            src_ref=rmine,
            dst_ref=rbuf,
            send_sem=swr_send.at[0],
            recv_sem=swr_recv.at[0],
            device_id=(mate_grp, mate_tok),
            device_id_type=MESH,
        )

    def ring(way, step, sub):
        origin = lax.rem(z + (NZ - step if way == 0 else step), NZ)
        block = xall.at[core * NZ + origin, rows_of(sub)]
        return pltpu.make_async_remote_copy(
            src_ref=block,
            dst_ref=block,
            send_sem=ring_send.at[way, step, sub],
            recv_sem=ring_recv.at[way, step, sub],
            device_id=(g, up_tok if way == 0 else down_tok),
            device_id_type=MESH,
        )

    def wait_ring(way, step, sub):
        origin = lax.rem(z + (NZ - step if way == 0 else step), NZ)
        block = xall.at[core * NZ + origin, rows_of(sub)]
        pltpu.make_async_copy(block, block, ring_recv.at[way, step - 1, sub]).wait()

    def share(origin, sub):
        block = xall.at[core * NZ + origin, rows_of(sub)]
        return pltpu.make_async_remote_copy(
            src_ref=block,
            dst_ref=block,
            send_sem=sib_send.at[origin, sub],
            recv_sem=sib_recv.at[origin, sub],
            device_id=(sib_grp, t),
            device_id_type=MESH,
        )

    def origin_of(way, step):
        return lax.rem(z + (NZ - step if way == 0 else step), NZ)

    reach = (4 - core, 3 + core)

    new = lax.broadcasted_iota(jnp.int32, (BLK, BLK), 0)
    old = lax.broadcasted_iota(jnp.int32, (BLK, BLK), 1)
    source = (lax.rem(new // 2, 4)) * 32 + (new // 8) * 2 + lax.rem(new, 2)
    pick = jnp.where(old == source, 1.0, 0.0).astype(BF16)

    def prepare(sub):
        own = jnp.dot(
            pick[sub * SUB : (sub + 1) * SUB], tok_ref[...], preferred_element_type=F32
        )
        scale = lax.rsqrt(jnp.mean(own * own, axis=-1, keepdims=True) + 1e-06)
        made = (own * scale * (1.0 + mod_ref[1:2, :]) + mod_ref[0:1, :]).astype(BF16)

        @pl.when(swapped)
        def _():
            xown[rows_of(sub), :] = made

        @pl.when(jnp.logical_not(swapped))
        def _():
            xall[head, rows_of(sub), :] = made

    def depart(sub):
        ring(0, 0, sub).start()
        ring(1, 0, sub).start()
        share(z, sub).start()

    for sub in range(SUBS):
        prepare(sub)
        if sub == 0:
            pl.semaphore_wait(barrier, guests)

        @pl.when(swapped)
        def _():
            swap_x(sub).start()
            if sub < 2:
                swap_w(sub).start()

        @pl.when(jnp.logical_not(swapped))
        def _():
            depart(sub)

    load_lw.wait()
    own_rows = jnp.dot(pick, tok_ref[...], preferred_element_type=F32).astype(BF16)
    rmine[...] = jnp.dot(own_rows, lw[...], preferred_element_type=F32)

    @pl.when(swapped)
    def _():
        swap_w(2).start()
        swap_r().start()
        for sub in range(SUBS):
            wait_swap_x(sub)
            depart(sub)

    v2[:, HD:] = jnp.ones((v2.shape[0], HD), BF16)
    radd[...] = jnp.zeros_like(radd)
    qs[...] = jnp.zeros_like(qs)
    to = lax.broadcasted_iota(jnp.int32, (4 * BLK, 4 * BLK), 0)
    of = lax.broadcasted_iota(jnp.int32, (4 * BLK, 4 * BLK), 1)
    row, col = lax.rem(to // 4, 8), lax.rem(to, 4)
    phase = lax.rem(row, 2) * 2 + lax.rem(col, 2)
    order[...] = jnp.where(
        of == phase * BLK + (row // 2) * 32 + (col // 2) * FR + to // 32, 1.0, 0.0
    ).astype(BF16)

    load_ow.wait()
    scaled = (ow[...].astype(F32) * gate_ref[...]).astype(BF16).reshape(NZ * 32, 256)
    cols = pl.ds(pl.multiple_of(t * 256, 256), 256)
    part = jnp.dot(scaled, lw[cols, :], preferred_element_type=F32)
    msend[...] = part.astype(BF16).reshape(NZ, 32, LAT)

    def fold_copy(other):
        return pltpu.make_async_remote_copy(
            src_ref=msend.at[lax.rem(other, NZ)],
            dst_ref=mrecv.at[t],
            send_sem=m_send.at[other],
            recv_sem=m_recv.at[t],
            device_id=(g, other),
            device_id_type=MESH,
        )

    mrecv[t] = msend[z]

    def fold_send(step, carry):
        fold_copy(lax.rem(t + step, FR)).start()
        return carry

    lax.fori_loop(1, FR, fold_send, 0)

    def fold_wait(step, carry):
        other = lax.rem(t + step, FR)
        pltpu.make_async_copy(mrecv.at[other], mrecv.at[other], m_recv.at[other]).wait()
        return carry

    def fold_sent(step, carry):
        fold_copy(lax.rem(t + step, FR)).wait_send()
        return carry

    def fold_rows(which):
        return mfull.at[pl.ds(pl.multiple_of(which * 32, 32), 32)]

    def spread(step):
        return pltpu.make_async_remote_copy(
            src_ref=fold_rows(x),
            dst_ref=fold_rows(x),
            send_sem=mx_send.at[step],
            recv_sem=mx_recv.at[x],
            device_id=(y_hi * (2 * n_x) + lax.rem(x + step, n_x) * 2 + core, t),
            device_id_type=MESH,
        )

    def project(kind, origin):
        slot = kind * NZ + origin
        triple = jnp.dot(xall[slot], wv[...], preferred_element_type=F32)
        qs[pl.ds(slot, BLK, stride=FR), :] = triple[:, :HD]
        place = 2 * lax.rem(origin - z + NZ + 3, NZ) + jnp.where(kind == core, 0, 1)
        at = pl.ds(pl.multiple_of(place * BLK, BLK), BLK)
        kt[:, at] = triple[:, HD : 2 * HD].T.astype(BF16)
        v2[at, :HD] = triple[:, 2 * HD :].astype(BF16)

    def project_sib(origin):
        for sub in range(SUBS):
            block = xall.at[(1 - core) * NZ + origin, rows_of(sub)]
            pltpu.make_async_copy(block, block, sib_recv.at[origin, sub]).wait()
        project(1 - core, origin)

    def forward(step):
        for sub in range(SUBS):
            for way in range(2):

                @pl.when(step <= reach[way])
                def _():
                    wait_ring(way, step, sub)

                    @pl.when(step < reach[way])
                    def _():
                        ring(way, step, sub).start()

                    share(origin_of(way, step), sub).start()

    def both(step, work):
        def go(way, carry):
            work(lax.rem(z + NZ + (2 * way - 1) * step, NZ))
            return carry

        lax.fori_loop(0, 2, go, 0)

    forward(1)

    @pl.when(jnp.logical_not(swapped))
    def _():
        for k in range(3):
            load_w(k).wait()
        rbuf[...] = rmine[...]

    @pl.when(swapped)
    def _():
        for k in range(3):
            swap_w(k).wait_recv()
        pltpu.make_async_copy(rbuf, rbuf, swr_recv.at[0]).wait()

    def first(n, carry):
        project(core, lax.rem(z + NZ + lax.rem(n + 1, 3) - 1, NZ))
        return carry

    lax.fori_loop(0, 3, first, 0)
    project_sib(z)
    radd[pl.ds(head, BLK, stride=FR), :] = rbuf[...]
    lax.fori_loop(1, FR, fold_wait, 0)
    total = mrecv[0].astype(F32)
    for other in range(1, FR):
        total = total + mrecv[other].astype(F32)
    mfull[pl.ds(pl.multiple_of(x * 32, 32), 32), :] = total.astype(BF16)
    for step in range(1, 4):
        spread(step).start()

    forward(2)
    both(2, lambda origin: project(core, origin))
    both(1, project_sib)
    forward(3)
    both(3, lambda origin: project(core, origin))
    both(2, project_sib)
    both(3, project_sib)
    for step in range(1, 4):
        there = lax.rem(x + step, n_x)
        pltpu.make_async_copy(fold_rows(there), fold_rows(there), mx_recv.at[there]).wait()

    def early(query):
        scores = jnp.dot(query.astype(BF16), kt[:, :EARLY], preferred_element_type=F32)
        top = jnp.max(scores, axis=-1, keepdims=True)
        probs = jnp.exp2((scores - top) * EXP_SCALE).astype(BF16)
        return top, jnp.dot(probs, v2[:EARLY, :], preferred_element_type=F32)

    def attend_early(n, carry):
        at = pl.ds(pl.multiple_of(n * 256, 256), 256)
        top, summed = early(qs[at, :])
        tops[at, :] = jnp.broadcast_to(top, (256, HD))
        sums[at, :] = summed[:, :HD]
        weights[at, :] = summed[:, HD:]
        return carry

    lax.fori_loop(0, FR // 2, attend_early, 0)
    forward(4)
    last = lax.rem(z + 4, NZ)
    project(core, last)
    project_sib(last)

    late_rows = [pl.ds(kind * NZ + last, BLK, stride=FR) for kind in range(2)]
    top, summed = early(jnp.concatenate([qs[rows, :] for rows in late_rows], axis=0))
    for kind in range(2):
        piece = slice(kind * BLK, (kind + 1) * BLK)
        tops[late_rows[kind], :] = jnp.broadcast_to(top[piece], (BLK, HD))
        sums[late_rows[kind], :] = summed[piece, :HD]
        weights[late_rows[kind], :] = summed[piece, HD:]

    home = pair + y_lo

    def latent_copy(two):
        return pltpu.make_async_remote_copy(
            src_ref=lsend.at[two],
            dst_ref=lrecv.at[z],
            send_sem=l_send.at[two],
            recv_sem=l_recv.at[z],
            device_id=(home, two * 2 + core),
            device_id_type=MESH,
        )

    def to_sibling(two):
        return pltpu.make_async_remote_copy(
            src_ref=psend.at[two],
            dst_ref=precv.at[two],
            send_sem=p_send.at[two],
            recv_sem=p_recv.at[two],
            device_id=(sib_grp, t),
            device_id_type=MESH,
        )

    def is_self(two):
        return jnp.logical_and(home == g, two * 2 + core == t)

    def turn(n):
        return lax.rem(n + t // 2 + 1, FR // 2)

    def attend(n):
        two = turn(n)
        at = pl.ds(pl.multiple_of(two * 256, 256), 256)
        scores = jnp.dot(qs[at, :].astype(BF16), kt[:, EARLY:], preferred_element_type=F32)
        before = tops[at, :]
        top = jnp.maximum(before, jnp.max(scores, axis=-1, keepdims=True))
        shrink = jnp.exp2((before - top) * EXP_SCALE)
        both_tops = jnp.concatenate([top, top], axis=1)
        probs = jnp.exp2((scores - both_tops) * EXP_SCALE).astype(BF16)
        summed = jnp.dot(probs, v2[EARLY:, :], preferred_element_type=F32)
        values = sums[at, :] * shrink + summed[:, :HD]
        weight = weights[at, :] * shrink + summed[:, HD:]
        attended = (values / weight).astype(BF16)
        latent = jnp.dot(attended, mfull[...], preferred_element_type=F32) + radd[at, :]
        mine = jnp.where(core == 0, latent[:BLK], latent[BLK:])
        other = jnp.where(core == 0, latent[BLK:], latent[:BLK])
        psend[two] = other.astype(BF16)
        to_sibling(two).start()
        pmine[two] = mine

    def pass_on(n):
        two = turn(n)
        to_sibling(two).wait_recv()
        summed = (pmine[two] + precv[two].astype(F32)).astype(BF16)

        @pl.when(jnp.logical_not(is_self(two)))
        def _():
            lsend[two] = summed
            latent_copy(two).start()

        @pl.when(is_self(two))
        def _():
            lrecv[z] = summed

    attend(0)

    def attend_and_pass(n, carry):
        attend(n)
        pass_on(n - 1)
        return carry

    lax.fori_loop(1, FR // 2, attend_and_pass, 0)
    pass_on(FR // 2 - 1)

    def latent_wait(n, carry):
        here = jnp.logical_and(core == y_lo, lax.rem(t, 2) == core)

        @pl.when(jnp.logical_not(jnp.logical_and(here, n == z)))
        def _():
            pltpu.make_async_copy(lrecv.at[n], lrecv.at[n], l_recv.at[n]).wait()

        return carry

    lax.fori_loop(0, NZ, latent_wait, 0)
    tile = lrecv[0].astype(F32)
    for n in range(1, NZ):
        tile = tile + lrecv[n].astype(F32)
    ext[2:6, 2:4] = tile.astype(BF16).reshape(4, 2, FR, LAT)

    def halo(dg, dt):
        rows_src, rows_dst = {0: ((2, 4), (2, 4)), 1: ((4, 2), (0, 2)), -1: ((2, 2), (6, 2))}[dg]
        cols_dst = {0: 2, 1: 0, -1: 4}[dt]
        at = (dg + 1) * 3 + dt + 1
        return pltpu.make_async_remote_copy(
            src_ref=ext.at[pl.ds(*rows_src), pl.ds(2, 2)],
            dst_ref=ext.at[pl.ds(*rows_dst), pl.ds(cols_dst, 2)],
            send_sem=h_send.at[at],
            recv_sem=h_recv.at[at],
            device_id=(g + dg, t + dt),
            device_id_type=MESH,
        )

    def inside(dg, dt):
        ok = jnp.logical_and(g + dg >= 0, g + dg < n_g)
        return jnp.logical_and(ok, jnp.logical_and(t + dt >= 0, t + dt < FR))

    ways = [(dg, dt) for dg in (-1, 0, 1) for dt in (-1, 0, 1) if (dg, dt) != (0, 0)]
    for dg, dt in ways:

        @pl.when(inside(dg, dt))
        def _():
            halo(dg, dt).start()

    load_cw.wait()
    load_rw.wait()
    for dg, dt in ways:

        @pl.when(inside(-dg, -dt))
        def _():
            halo(dg, dt).wait_recv()

    def over_frames(three, rows):
        frame = lax.rem(lax.broadcasted_iota(jnp.int32, (rows, CH), 0), FR)
        before = pltpu.roll(three[0], 1, 0)
        after = pltpu.roll(three[2], rows - 1, 0)
        return (
            three[1]
            + jnp.where(frame > 0, before, 0.0)
            + jnp.where(frame < FR - 1, after, 0.0)
        )

    def silu(v):
        return v / (1.0 + jnp.exp(-v))

    views = [
        ext[b : b + 6, c : c + 4].reshape(24 * FR, LAT) for b in range(3) for c in range(3)
    ]
    cells = jnp.concatenate(views, axis=1)
    three = [jnp.dot(cells, cw[a], preferred_element_type=F32) for a in range(3)]
    made = silu(over_frames(three, 24 * FR) + cb_ref[...]).astype(BF16)
    coarse[...] = made.reshape(6, 4, FR, CH)

    @pl.when(g == 0)
    def _():
        coarse[0:1] = jnp.zeros((1, 4, FR, CH), BF16)

    @pl.when(g == n_g - 1)
    def _():
        coarse[5:6] = jnp.zeros((1, 4, FR, CH), BF16)

    @pl.when(t == 0)
    def _():
        coarse[:, 0:1] = jnp.zeros((6, 1, FR, CH), BF16)

    @pl.when(t == FR - 1)
    def _():
        coarse[:, 3:4] = jnp.zeros((6, 1, FR, CH), BF16)

    rows = 8 * FR
    for p in range(2):
        for q in range(2):
            for b in range(3):
                for c in range(3):
                    r0 = 1 + (p + b - 1) // 2
                    c0 = 1 + (q + c - 1) // 2
                    at = (p * 2 + q) * rows
                    k = (b * 3 + c) * CH
                    cols2[at : at + rows, k : k + CH] = coarse[
                        r0 : r0 + 4, c0 : c0 + 2
                    ].reshape(rows, CH)
    three = [jnp.dot(cols2[...], rw[a], preferred_element_type=F32) for a in range(3)]
    mixed = over_frames(three, 4 * rows)
    center = coarse[1:5, 1:3].reshape(rows, CH).astype(F32)
    center = jnp.concatenate([center] * 4, axis=0)
    result = silu(center + mixed + rb_ref[...]).astype(BF16)
    out_ref[...] = jnp.dot(order[...], result, preferred_element_type=F32).astype(BF16)

    for sub in range(SUBS):

        @pl.when(swapped)
        def _():
            swap_x(sub).wait_send()

        for way in range(2):
            for step in range(4):

                @pl.when(step < reach[way])
                def _():
                    ring(way, step, sub).wait_send()

        for origin in range(NZ):
            share(origin, sub).wait_send()

    @pl.when(swapped)
    def _():
        for k in range(3):
            swap_w(k).wait_send()
        swap_r().wait_send()

    lax.fori_loop(1, FR, fold_sent, 0)
    for step in range(1, 4):
        spread(step).wait_send()

    def latent_sent(two, carry):
        to_sibling(two).wait_send()

        @pl.when(jnp.logical_not(is_self(two)))
        def _():
            latent_copy(two).wait_send()

        return carry

    lax.fori_loop(0, FR // 2, latent_sent, 0)
    for dg, dt in ways:

        @pl.when(inside(dg, dt))
        def _():
            halo(dg, dt).wait_send()


def shards(
    tokens,
    modulation,
    triple_weight,
    out_weight,
    gate,
    latent_weight,
    conv_weight,
    conv_bias,
    res_weight,
    res_bias,
):
    vmem = pl.BlockSpec(memory_space=pltpu.VMEM)
    hbm = pl.BlockSpec(memory_space=pl.ANY)
    dma = pltpu.SemaphoreType.DMA
    out = pl.pallas_call(
        kernel,
        out_shape=jax.ShapeDtypeStruct((4 * BLK, CH), BF16),
        in_specs=[vmem, vmem, hbm, hbm, vmem, hbm, hbm, vmem, hbm, vmem],
        out_specs=vmem,
        scratch_shapes=[
            pltpu.VMEM((FR, BLK, D), BF16),
            pltpu.VMEM((BLK, D), BF16),
            pltpu.VMEM((D, 3 * HD), BF16),
            pltpu.VMEM((D, LAT), BF16),
            pltpu.VMEM((NZ, 32, 256), BF16),
            pltpu.VMEM((3, 9 * LAT, CH), BF16),
            pltpu.VMEM((3, 9 * CH, CH), BF16),
            pltpu.VMEM((FR * BLK, HD), F32),
            pltpu.VMEM((HD, FR * BLK), BF16),
            pltpu.VMEM((FR * BLK, 2 * HD), BF16),
            pltpu.VMEM((FR * BLK, LAT), F32),
            pltpu.VMEM((BLK, LAT), F32),
            pltpu.VMEM((BLK, LAT), F32),
            pltpu.VMEM((FR, 32, LAT), BF16),
            pltpu.VMEM((NZ, 32, LAT), BF16),
            pltpu.VMEM((HD, LAT), BF16),
            pltpu.VMEM((NZ, BLK, LAT), BF16),
            pltpu.VMEM((NZ, BLK, LAT), BF16),
            pltpu.VMEM((NZ, BLK, LAT), BF16),
            pltpu.VMEM((NZ, BLK, LAT), BF16),
            pltpu.VMEM((NZ, BLK, LAT), F32),
            pltpu.VMEM((FR * BLK, HD), F32),
            pltpu.VMEM((FR * BLK, HD), F32),
            pltpu.VMEM((FR * BLK, HD), F32),
            pltpu.VMEM((4 * BLK, 4 * BLK), BF16),
            pltpu.VMEM((8, 6, FR, LAT), BF16),
            pltpu.VMEM((6, 4, FR, CH), BF16),
            pltpu.VMEM((4 * 8 * FR, 9 * CH), BF16),
            dma((4,)),
            dma((3,)),
            dma((SUBS,)), dma((SUBS,)),
            dma((3,)), dma((3,)),
            dma((1,)), dma((1,)),
            dma((2, 4, SUBS)), dma((2, 4, SUBS)),
            dma((NZ, SUBS)), dma((NZ, SUBS)),
            dma((FR,)), dma((FR,)),
            dma((4,)), dma((4,)),
            dma((NZ,)), dma((NZ,)),
            dma((NZ,)), dma((NZ,)),
            dma((9,)), dma((9,)),
        ],
        compiler_params=pltpu.CompilerParams(
            collective_id=0, has_side_effects=True, vmem_limit_bytes=60 * 2**20
        ),
        cost_estimate=pl.CostEstimate(
            flops=13 * 10**9, bytes_accessed=14 * 10**6, transcendentals=5 * 10**6
        ),
    )(
        tokens[0],
        modulation,
        triple_weight.transpose(1, 0, 2),
        out_weight.reshape(2, NZ, 4, 32, 256),
        gate.reshape(1, 256),
        latent_weight,
        conv_weight.reshape(3, 9 * LAT, CH),
        conv_bias.reshape(1, CH),
        res_weight.reshape(3, 9 * CH, CH),
        res_bias.reshape(1, CH),
    )
    return out.reshape(FR, 8, 4, CH)


def solution(mesh):
    placed = (
        P("grp", "tok", None),
        P(),
        P(None, None, "tok"),
        P(None, "tok"),
        P("tok"),
        P(),
        P(),
        P(),
        P(),
        P(),
    )
    return jax.shard_map(
        shards, mesh=mesh, in_specs=placed, out_specs=P(None, "grp", "tok", None), check_vma=False
    )
```

```python
import math

import jax
import jax.numpy as jnp
from jax import lax
from jax.experimental import pallas as pl
from jax.experimental.pallas import tpu as pltpu
from jax.sharding import PartitionSpec as P

MESH = pl.DeviceIdType.MESH
F32 = jnp.float32
BF16 = jnp.bfloat16

D = 4096
HD = 128
FR = 16
BLK = 128
SUBS = 4
SUB = BLK // SUBS
LAT = 128
CH = 256
NZ = 8
EXP_SCALE = HD ** (-0.5) * math.log2(math.e)


def kernel(
    tok_ref, mod_ref, w_hbm, ow_hbm, gate_ref, lw_hbm, cw_hbm, cb_ref, rw_hbm, rb_ref,
    out_ref,
    xall, xown, wv, lw, ow, cw, rw, qs, kt, v2, rmine, rbuf, mrecv, msend, mfull,
    lsend, lrecv, psend, precv, lat, tops, sums, order, ext, coarse, cols2,
    local_sem, wloc_sem, swx_send, swx_recv, sww_send, sww_recv, swr_send, swr_recv,
    ring_send, ring_recv, sib_send, sib_recv, m_send, m_recv, mx_send, mx_recv,
    l_send, l_recv, p_send, p_recv, h_send, h_recv,
):
    g = lax.axis_index("grp")
    t = lax.axis_index("tok")
    n_x = lax.axis_size("grp") // 4
    n_g = lax.axis_size("grp")
    core = lax.rem(g, 2)
    pair = g - core
    x = lax.rem(g // 2, n_x)
    y_hi = g // (2 * n_x)
    y_lo = t // NZ
    z = lax.rem(t, NZ)
    swapped = core != y_lo
    head = core * NZ + z
    mate_grp = pair + y_lo
    far_grp = (1 - y_hi) * (2 * n_x) + x * 2 + y_lo
    mate_tok = head
    sib_grp = pair + 1 - core
    up_tok = y_lo * NZ + lax.rem(z + 1, NZ)
    down_tok = y_lo * NZ + lax.rem(z + NZ - 1, NZ)
    outer = g + 2 * core - 1
    has_outer = jnp.logical_and(outer >= 0, outer < n_g)

    ext[...] = jnp.zeros_like(ext)

    barrier = pltpu.get_barrier_semaphore()

    def greet(grp, tok):
        pl.semaphore_signal(barrier, inc=1, device_id=(grp, tok), device_id_type=MESH)

    def greet_row(step, carry):
        other = lax.rem(t + step, FR)

        @pl.when(step > 0)
        def _():
            greet(g, other)

        greet(sib_grp, other)
        return carry

    lax.fori_loop(0, FR, greet_row, 0)
    for step in range(1, 4):
        greet(y_hi * (2 * n_x) + lax.rem(x + step, n_x) * 2 + core, t)

    @pl.when(swapped)
    def _():
        greet(far_grp, mate_tok)

    @pl.when(has_outer)
    def _():
        greet(outer, t)

        @pl.when(t > 0)
        def _():
            greet(outer, t - 1)

        @pl.when(t < FR - 1)
        def _():
            greet(outer, t + 1)

    guests = 2 * FR - 1 + 3 + jnp.where(swapped, 1, 0) + jnp.where(
        has_outer, 1 + jnp.where(t > 0, 1, 0) + jnp.where(t < FR - 1, 1, 0), 0
    )

    load_lw = pltpu.make_async_copy(lw_hbm, lw, local_sem.at[0])
    load_ow = pltpu.make_async_copy(ow_hbm.at[core, :, x], ow, local_sem.at[1])
    load_cw = pltpu.make_async_copy(cw_hbm, cw, local_sem.at[2])
    load_rw = pltpu.make_async_copy(rw_hbm, rw, local_sem.at[3])
    load_lw.start()
    load_ow.start()

    def third(k):
        return wv.at[:, pl.ds(k * HD, HD)]

    def load_w(k):
        return pltpu.make_async_copy(w_hbm.at[k], third(k), wloc_sem.at[k])

    @pl.when(jnp.logical_not(swapped))
    def _():
        for k in range(3):
            load_w(k).start()

    load_cw.start()
    load_rw.start()

    def rows_of(sub):
        return pl.ds(sub * SUB, SUB)

    def swap_x(sub):
        return pltpu.make_async_remote_copy(
            src_ref=xown.at[rows_of(sub)],
            dst_ref=xall.at[t, rows_of(sub)],
            send_sem=swx_send.at[sub],
            recv_sem=swx_recv.at[sub],
            device_id=(mate_grp, mate_tok),
            device_id_type=MESH,
        )

    def wait_swap_x(sub):
        pltpu.make_async_copy(
            xall.at[head, rows_of(sub)], xall.at[head, rows_of(sub)], swx_recv.at[sub]
        ).wait()

    def swap_w(k):
        return pltpu.make_async_remote_copy(
            src_ref=w_hbm.at[k],
            dst_ref=third(k),
            send_sem=sww_send.at[k],
            recv_sem=sww_recv.at[k],
            device_id=(mate_grp if k == 2 else far_grp, mate_tok),
            device_id_type=MESH,
        )

    def swap_r():
        return pltpu.make_async_remote_copy(
            src_ref=rmine,
            dst_ref=rbuf,
            send_sem=swr_send.at[0],
            recv_sem=swr_recv.at[0],
            device_id=(mate_grp, mate_tok),
            device_id_type=MESH,
        )

    def ring(way, step, sub):
        origin = lax.rem(z + (NZ - step if way == 0 else step), NZ)
        block = xall.at[core * NZ + origin, rows_of(sub)]
        return pltpu.make_async_remote_copy(
            src_ref=block,
            dst_ref=block,
            send_sem=ring_send.at[way, step, sub],
            recv_sem=ring_recv.at[way, step, sub],
            device_id=(g, up_tok if way == 0 else down_tok),
            device_id_type=MESH,
        )

    def wait_ring(way, step, sub):
        origin = lax.rem(z + (NZ - step if way == 0 else step), NZ)
        block = xall.at[core * NZ + origin, rows_of(sub)]
        pltpu.make_async_copy(block, block, ring_recv.at[way, step - 1, sub]).wait()

    def share(origin, sub):
        block = xall.at[core * NZ + origin, rows_of(sub)]
        return pltpu.make_async_remote_copy(
            src_ref=block,
            dst_ref=block,
            send_sem=sib_send.at[origin, sub],
            recv_sem=sib_recv.at[origin, sub],
            device_id=(sib_grp, t),
            device_id_type=MESH,
        )

    def origin_of(way, step):
        return lax.rem(z + (NZ - step if way == 0 else step), NZ)

    reach = (4 - core, 3 + core)

    new = lax.broadcasted_iota(jnp.int32, (BLK, BLK), 0)
    old = lax.broadcasted_iota(jnp.int32, (BLK, BLK), 1)
    source = (lax.rem(new // 2, 4)) * 32 + (new // 8) * 2 + lax.rem(new, 2)
    pick = jnp.where(old == source, 1.0, 0.0).astype(BF16)

    def prepare(sub):
        own = jnp.dot(
            pick[sub * SUB : (sub + 1) * SUB], tok_ref[...], preferred_element_type=F32
        )
        scale = lax.rsqrt(jnp.mean(own * own, axis=-1, keepdims=True) + 1e-06)
        made = (own * scale * (1.0 + mod_ref[1:2, :]) + mod_ref[0:1, :]).astype(BF16)

        @pl.when(swapped)
        def _():
            xown[rows_of(sub), :] = made

        @pl.when(jnp.logical_not(swapped))
        def _():
            xall[head, rows_of(sub), :] = made

    def depart(sub):
        ring(0, 0, sub).start()
        ring(1, 0, sub).start()
        share(z, sub).start()

    for sub in range(SUBS):
        prepare(sub)
        if sub == 0:
            pl.semaphore_wait(barrier, guests)

        @pl.when(swapped)
        def _():
            swap_x(sub).start()
            if sub < 2:
                swap_w(sub).start()

        @pl.when(jnp.logical_not(swapped))
        def _():
            depart(sub)

    load_lw.wait()
    own_rows = jnp.dot(pick, tok_ref[...], preferred_element_type=F32).astype(BF16)
    rmine[...] = jnp.dot(own_rows, lw[...], preferred_element_type=F32)

    @pl.when(swapped)
    def _():
        swap_w(2).start()
        swap_r().start()
        for sub in range(SUBS):
            wait_swap_x(sub)
            depart(sub)

    def fold_copy(other):
        return pltpu.make_async_remote_copy(
            src_ref=msend.at[lax.rem(other, NZ)],
            dst_ref=mrecv.at[t],
            send_sem=m_send.at[other],
            recv_sem=m_recv.at[t],
            device_id=(g, other),
            device_id_type=MESH,
        )

    def fold_wait(step, carry):
        other = lax.rem(t + step, FR)
        pltpu.make_async_copy(mrecv.at[other], mrecv.at[other], m_recv.at[other]).wait()
        return carry

    def fold_sent(step, carry):
        fold_copy(lax.rem(t + step, FR)).wait_send()
        return carry

    def fold_rows(which):
        return mfull.at[pl.ds(pl.multiple_of(which * 32, 32), 32)]

    def spread(step):
        return pltpu.make_async_remote_copy(
            src_ref=fold_rows(x),
            dst_ref=fold_rows(x),
            send_sem=mx_send.at[step],
            recv_sem=mx_recv.at[x],
            device_id=(y_hi * (2 * n_x) + lax.rem(x + step, n_x) * 2 + core, t),
            device_id_type=MESH,
        )

    def place_of(p):
        if isinstance(p, int):
            table = [(k, o) for k in (0, 1) for o in (0, 1, -1)]
            for far in (2, 3):
                table += [(k, o) for k in (0, 1) for o in (far, -far)]
            return (table + [(0, 4), (1, 4)])[p]
        stage, p = p
        if stage == 0:
            return p // 3, lax.rem(p + 1, 3) - 1
        if stage < 3:
            return (p - 4 * stage - 2) // 2, (stage + 1) * (1 - 2 * lax.rem(p, 2))
        return p - 14, 4

    def slot_of(p):
        kind, offset = place_of(p)
        return jnp.where(kind == 0, core, 1 - core) * NZ + lax.rem(z + NZ + offset, NZ)

    def project(stage, low, high):
        def one(p, carry):
            kind, offset = place_of((stage, p))
            origin = lax.rem(z + NZ + offset, NZ)

            @pl.when(kind == 1)
            def _():
                for sub in range(SUBS):
                    block = xall.at[(1 - core) * NZ + origin, rows_of(sub)]
                    pltpu.make_async_copy(block, block, sib_recv.at[origin, sub]).wait()

            triple = jnp.dot(xall[slot_of((stage, p))], wv[...], preferred_element_type=F32)
            qs[p] = (triple[:, :HD] * EXP_SCALE).astype(BF16)
            at = pl.ds(pl.multiple_of(p * BLK, BLK), BLK)
            kt[:, at] = triple[:, HD : 2 * HD].T.astype(BF16)
            v2[at, :HD] = triple[:, 2 * HD :].astype(BF16)
            return carry

        lax.fori_loop(low, high, one, 0)

    def forward(step, sub):
        for way in range(2):

            @pl.when(step <= reach[way])
            def _():
                wait_ring(way, step, sub)

                @pl.when(step < reach[way])
                def _():
                    ring(way, step, sub).start()

                share(origin_of(way, step), sub).start()

    def meet(query, low, high, before=None):
        keys = slice(low * BLK, high * BLK)
        scores = jnp.dot(query, kt[:, keys], preferred_element_type=F32)
        top = jnp.max(scores, axis=-1, keepdims=True)
        top = jnp.broadcast_to(top, (query.shape[0], HD))
        if before is not None:
            top = jnp.maximum(before, top)
        probs = jnp.exp2(scores - jnp.concatenate([top] * (high - low), axis=1))
        return top, jnp.dot(probs.astype(BF16), v2[keys, :], preferred_element_type=F32)

    def merged(summed, before, top, added):
        shrink = jnp.exp2(before - top)
        return summed * jnp.concatenate([shrink, shrink], axis=1) + added

    def fresh(low, high, upto):
        def one(n, carry):
            at = pl.ds(2 * n, 2)
            top, summed = meet(qs[at].reshape(2 * BLK, HD), 0, upto)
            tops[at] = top.reshape(2, BLK, HD)
            sums[at] = summed.reshape(2, BLK, 2 * HD)
            return carry

        lax.fori_loop(low // 2, high // 2, one, 0)

    def update(rows, low, high):
        def one(n, carry):
            at = pl.ds(2 * n, 2)
            before = tops[at].reshape(2 * BLK, HD)
            top, added = meet(qs[at].reshape(2 * BLK, HD), low, high, before)
            summed = merged(sums[at].reshape(2 * BLK, 2 * HD), before, top, added)
            tops[at] = top.reshape(2, BLK, HD)
            sums[at] = summed.reshape(2, BLK, 2 * HD)
            return carry

        lax.fori_loop(0, rows // 2, one, 0)

    forward(1, 0)
    v2[:, HD:] = jnp.ones((v2.shape[0], HD), BF16)
    to = lax.broadcasted_iota(jnp.int32, (4 * BLK, 4 * BLK), 0)
    of = lax.broadcasted_iota(jnp.int32, (4 * BLK, 4 * BLK), 1)
    row, col = lax.rem(to // 4, 8), lax.rem(to, 4)
    phase = lax.rem(row, 2) * 2 + lax.rem(col, 2)
    order[...] = jnp.where(
        of == phase * BLK + (row // 2) * 32 + (col // 2) * FR + to // 32, 1.0, 0.0
    ).astype(BF16)

    forward(1, 1)
    load_ow.wait()
    scaled = (ow[...].astype(F32) * gate_ref[...]).astype(BF16).reshape(NZ * 32, 256)
    cols = pl.ds(pl.multiple_of(t * 256, 256), 256)
    part = jnp.dot(scaled, lw[cols, :], preferred_element_type=F32)
    msend[...] = part.astype(BF16).reshape(NZ, 32, LAT)

    mrecv[t] = msend[z]

    def fold_send(step, carry):
        fold_copy(lax.rem(t + step, FR)).start()
        return carry

    lax.fori_loop(1, FR, fold_send, 0)

    forward(1, 2)
    forward(1, 3)
    forward(2, 0)

    @pl.when(jnp.logical_not(swapped))
    def _():
        for k in range(3):
            load_w(k).wait()
        rbuf[...] = rmine[...]

    @pl.when(swapped)
    def _():
        for k in range(3):
            swap_w(k).wait_recv()
        pltpu.make_async_copy(rbuf, rbuf, swr_recv.at[0]).wait()

    project(0, 0, 2)
    forward(2, 1)
    project(0, 2, 4)
    forward(2, 2)
    project(0, 4, 6)
    forward(2, 3)
    fresh(0, 6, 6)

    forward(3, 0)
    project(1, 6, 8)
    lax.fori_loop(1, FR, fold_wait, 0)
    total = mrecv[0].astype(F32)
    for other in range(1, FR):
        total = total + mrecv[other].astype(F32)
    mfull[pl.ds(pl.multiple_of(x * 32, 32), 32), :] = total.astype(BF16)
    for step in range(1, 4):
        spread(step).start()
    forward(3, 1)
    project(1, 8, 10)
    forward(3, 2)
    update(6, 6, 10)
    forward(3, 3)
    fresh(6, 10, 10)

    forward(4, 0)
    project(2, 10, 12)
    forward(4, 1)
    project(2, 12, 14)
    forward(4, 2)
    update(10, 10, 14)
    fresh(10, 14, 14)
    for step in range(1, 4):
        there = lax.rem(x + step, n_x)
        pltpu.make_async_copy(fold_rows(there), fold_rows(there), mx_recv.at[there]).wait()
    forward(4, 3)
    project(3, 14, 16)

    home = pair + y_lo

    def latent_copy(two):
        return pltpu.make_async_remote_copy(
            src_ref=lsend.at[two],
            dst_ref=lrecv.at[z],
            send_sem=l_send.at[two],
            recv_sem=l_recv.at[z],
            device_id=(home, two * 2 + core),
            device_id_type=MESH,
        )

    def to_sibling(two):
        return pltpu.make_async_remote_copy(
            src_ref=psend.at[two],
            dst_ref=precv.at[two],
            send_sem=p_send.at[two],
            recv_sem=p_recv.at[two],
            device_id=(sib_grp, t),
            device_id_type=MESH,
        )

    def is_self(two):
        return jnp.logical_and(home == g, two * 2 + core == t)

    def half_of(two, which):
        return lat[pl.ds(pl.multiple_of(two * 256 + which * BLK, BLK), BLK), :]

    H = BLK // 2

    def finish(half):
        part = pl.ds(half * H, H)
        before = tops[0:14, part].reshape(14 * H, HD)
        top, added = meet(qs[0:14, part].reshape(14 * H, HD), 14, 16, before)
        older = merged(sums[0:14, part].reshape(14 * H, 2 * HD), before, top, added)
        newer = meet(qs[14:16, part].reshape(2 * H, HD), 0, 16)[1]
        summed = jnp.concatenate([older, newer], axis=0)
        attended = (summed[:, :HD] / summed[:, HD:]).astype(BF16)
        latent = jnp.dot(attended, mfull[...], preferred_element_type=F32)
        for p in range(16):
            piece = latent[p * H : (p + 1) * H]
            if p == 0:
                piece = piece + rbuf[part, :]
            lat[pl.ds(slot_of(p) + half * H * FR, H, stride=FR), :] = piece

    def hand_over(n, carry):
        psend[n] = half_of(n, 1 - core).astype(BF16)
        to_sibling(n).start()
        return carry

    def pass_on(n, carry):
        two = (n // 4) * 4 + lax.rem(n + z, 4)
        to_sibling(two).wait_recv()
        summed = (half_of(two, core) + precv[two].astype(F32)).astype(BF16)

        @pl.when(jnp.logical_not(is_self(two)))
        def _():
            lsend[two] = summed
            latent_copy(two).start()

        @pl.when(is_self(two))
        def _():
            lrecv[z] = summed

        return carry

    for half in range(2):
        finish(half)
        lax.fori_loop(half * 4, half * 4 + 4, hand_over, 0)
        lax.fori_loop(half * 4, half * 4 + 4, pass_on, 0)

    def latent_wait(n, carry):
        here = jnp.logical_and(core == y_lo, lax.rem(t, 2) == core)

        @pl.when(jnp.logical_not(jnp.logical_and(here, n == z)))
        def _():
            pltpu.make_async_copy(lrecv.at[n], lrecv.at[n], l_recv.at[n]).wait()

        return carry

    lax.fori_loop(0, NZ, latent_wait, 0)
    tile = lrecv[0].astype(F32)
    for n in range(1, NZ):
        tile = tile + lrecv[n].astype(F32)
    ext[2:6, 2:4] = tile.astype(BF16).reshape(4, 2, FR, LAT)

    def halo(dg, dt):
        rows_src, rows_dst = {0: ((2, 4), (2, 4)), 1: ((4, 2), (0, 2)), -1: ((2, 2), (6, 2))}[dg]
        cols_dst = {0: 2, 1: 0, -1: 4}[dt]
        at = (dg + 1) * 3 + dt + 1
        return pltpu.make_async_remote_copy(
            src_ref=ext.at[pl.ds(*rows_src), pl.ds(2, 2)],
            dst_ref=ext.at[pl.ds(*rows_dst), pl.ds(cols_dst, 2)],
            send_sem=h_send.at[at],
            recv_sem=h_recv.at[at],
            device_id=(g + dg, t + dt),
            device_id_type=MESH,
        )

    def inside(dg, dt):
        ok = jnp.logical_and(g + dg >= 0, g + dg < n_g)
        return jnp.logical_and(ok, jnp.logical_and(t + dt >= 0, t + dt < FR))

    ways = [(dg, dt) for dg in (-1, 0, 1) for dt in (-1, 0, 1) if (dg, dt) != (0, 0)]
    for dg, dt in ways:

        @pl.when(inside(dg, dt))
        def _():
            halo(dg, dt).start()

    load_cw.wait()
    load_rw.wait()
    for dg, dt in ways:

        @pl.when(inside(-dg, -dt))
        def _():
            halo(dg, dt).wait_recv()

    def over_frames(three, rows):
        frame = lax.rem(lax.broadcasted_iota(jnp.int32, (rows, CH), 0), FR)
        before = pltpu.roll(three[0], 1, 0)
        after = pltpu.roll(three[2], rows - 1, 0)
        return (
            three[1]
            + jnp.where(frame > 0, before, 0.0)
            + jnp.where(frame < FR - 1, after, 0.0)
        )

    def silu(v):
        return v / (1.0 + jnp.exp(-v))

    views = [
        ext[b : b + 6, c : c + 4].reshape(24 * FR, LAT) for b in range(3) for c in range(3)
    ]
    cells = jnp.concatenate(views, axis=1)
    three = [jnp.dot(cells, cw[a], preferred_element_type=F32) for a in range(3)]
    made = silu(over_frames(three, 24 * FR) + cb_ref[...]).astype(BF16)
    coarse[...] = made.reshape(6, 4, FR, CH)

    @pl.when(g == 0)
    def _():
        coarse[0:1] = jnp.zeros((1, 4, FR, CH), BF16)

    @pl.when(g == n_g - 1)
    def _():
        coarse[5:6] = jnp.zeros((1, 4, FR, CH), BF16)

    @pl.when(t == 0)
    def _():
        coarse[:, 0:1] = jnp.zeros((6, 1, FR, CH), BF16)

    @pl.when(t == FR - 1)
    def _():
        coarse[:, 3:4] = jnp.zeros((6, 1, FR, CH), BF16)

    rows = 8 * FR
    for p in range(2):
        for q in range(2):
            for b in range(3):
                for c in range(3):
                    r0 = 1 + (p + b - 1) // 2
                    c0 = 1 + (q + c - 1) // 2
                    at = (p * 2 + q) * rows
                    k = (b * 3 + c) * CH
                    cols2[at : at + rows, k : k + CH] = coarse[
                        r0 : r0 + 4, c0 : c0 + 2
                    ].reshape(rows, CH)
    three = [jnp.dot(cols2[...], rw[a], preferred_element_type=F32) for a in range(3)]
    mixed = over_frames(three, 4 * rows)
    center = coarse[1:5, 1:3].reshape(rows, CH).astype(F32)
    center = jnp.concatenate([center] * 4, axis=0)
    result = silu(center + mixed + rb_ref[...]).astype(BF16)
    out_ref[...] = jnp.dot(order[...], result, preferred_element_type=F32).astype(BF16)

    for sub in range(SUBS):

        @pl.when(swapped)
        def _():
            swap_x(sub).wait_send()

        for way in range(2):
            for step in range(4):

                @pl.when(step < reach[way])
                def _():
                    ring(way, step, sub).wait_send()

        for origin in range(NZ):
            share(origin, sub).wait_send()

    @pl.when(swapped)
    def _():
        for k in range(3):
            swap_w(k).wait_send()
        swap_r().wait_send()

    lax.fori_loop(1, FR, fold_sent, 0)
    for step in range(1, 4):
        spread(step).wait_send()

    def latent_sent(two, carry):
        to_sibling(two).wait_send()

        @pl.when(jnp.logical_not(is_self(two)))
        def _():
            latent_copy(two).wait_send()

        return carry

    lax.fori_loop(0, FR // 2, latent_sent, 0)
    for dg, dt in ways:

        @pl.when(inside(dg, dt))
        def _():
            halo(dg, dt).wait_send()


def shards(
    tokens,
    modulation,
    triple_weight,
    out_weight,
    gate,
    latent_weight,
    conv_weight,
    conv_bias,
    res_weight,
    res_bias,
):
    vmem = pl.BlockSpec(memory_space=pltpu.VMEM)
    hbm = pl.BlockSpec(memory_space=pl.ANY)
    dma = pltpu.SemaphoreType.DMA
    out = pl.pallas_call(
        kernel,
        out_shape=jax.ShapeDtypeStruct((4 * BLK, CH), BF16),
        in_specs=[vmem, vmem, hbm, hbm, vmem, hbm, hbm, vmem, hbm, vmem],
        out_specs=vmem,
        scratch_shapes=[
            pltpu.VMEM((FR, BLK, D), BF16),
            pltpu.VMEM((BLK, D), BF16),
            pltpu.VMEM((D, 3 * HD), BF16),
            pltpu.VMEM((D, LAT), BF16),
            pltpu.VMEM((NZ, 32, 256), BF16),
            pltpu.VMEM((3, 9 * LAT, CH), BF16),
            pltpu.VMEM((3, 9 * CH, CH), BF16),
            pltpu.VMEM((FR, BLK, HD), BF16),
            pltpu.VMEM((HD, FR * BLK), BF16),
            pltpu.VMEM((FR * BLK, 2 * HD), BF16),
            pltpu.VMEM((BLK, LAT), F32),
            pltpu.VMEM((BLK, LAT), F32),
            pltpu.VMEM((FR, 32, LAT), BF16),
            pltpu.VMEM((NZ, 32, LAT), BF16),
            pltpu.VMEM((HD, LAT), BF16),
            pltpu.VMEM((NZ, BLK, LAT), BF16),
            pltpu.VMEM((NZ, BLK, LAT), BF16),
            pltpu.VMEM((NZ, BLK, LAT), BF16),
            pltpu.VMEM((NZ, BLK, LAT), BF16),
            pltpu.VMEM((FR * BLK, LAT), F32),
            pltpu.VMEM((FR, BLK, HD), F32),
            pltpu.VMEM((FR, BLK, 2 * HD), F32),
            pltpu.VMEM((4 * BLK, 4 * BLK), BF16),
            pltpu.VMEM((8, 6, FR, LAT), BF16),
            pltpu.VMEM((6, 4, FR, CH), BF16),
            pltpu.VMEM((4 * 8 * FR, 9 * CH), BF16),
            dma((4,)),
            dma((3,)),
            dma((SUBS,)), dma((SUBS,)),
            dma((3,)), dma((3,)),
            dma((1,)), dma((1,)),
            dma((2, 4, SUBS)), dma((2, 4, SUBS)),
            dma((NZ, SUBS)), dma((NZ, SUBS)),
            dma((FR,)), dma((FR,)),
            dma((4,)), dma((4,)),
            dma((NZ,)), dma((NZ,)),
            dma((NZ,)), dma((NZ,)),
            dma((9,)), dma((9,)),
        ],
        compiler_params=pltpu.CompilerParams(
            collective_id=0, has_side_effects=True, vmem_limit_bytes=60 * 2**20
        ),
        cost_estimate=pl.CostEstimate(
            flops=13 * 10**9, bytes_accessed=14 * 10**6, transcendentals=5 * 10**6
        ),
    )(
        tokens[0],
        modulation,
        triple_weight.transpose(1, 0, 2),
        out_weight.reshape(2, NZ, 4, 32, 256),
        gate.reshape(1, 256),
        latent_weight,
        conv_weight.reshape(3, 9 * LAT, CH),
        conv_bias.reshape(1, CH),
        res_weight.reshape(3, 9 * CH, CH),
        res_bias.reshape(1, CH),
    )
    return out.reshape(FR, 8, 4, CH)


def solution(mesh):
    placed = (
        P("grp", "tok", None),
        P(),
        P(None, None, "tok"),
        P(None, "tok"),
        P("tok"),
        P(),
        P(),
        P(),
        P(),
        P(),
    )
    return jax.shard_map(
        shards, mesh=mesh, in_specs=placed, out_specs=P(None, "grp", "tok", None), check_vma=False
    )
```

```python
import math

import jax
import jax.numpy as jnp
from jax import lax
from jax.experimental import pallas as pl
from jax.experimental.pallas import tpu as pltpu
from jax.sharding import PartitionSpec as P

MESH = pl.DeviceIdType.MESH
F32 = jnp.float32
BF16 = jnp.bfloat16

D = 4096
HD = 128
FR = 16
BLK = 128
SUBS = 4
SUB = BLK // SUBS
LAT = 128
CH = 256
NZ = 8
EXP_SCALE = HD ** (-0.5) * math.log2(math.e)


def kernel(
    tok_hbm, mod_hbm, w_hbm, ow_hbm, gate_hbm, lw_hbm, cw_hbm, cb_hbm, rw_hbm, rb_hbm,
    out_ref,
    tok_ref, mod_ref, gate_ref, cb_ref, rb_ref, xall, xown, wv, lw, ow, cw, rw, qs, kt, v2, rmine, rbuf, mrecv, msend, mfull,
    lsend, lrecv, psend, precv, lat, tops, sums, order, ext, coarse, wc,
    early_sem, local_sem, wloc_sem, swx_send, swx_recv, sww_send, sww_recv, swr_send, swr_recv,
    ring_send, ring_recv, sib_send, sib_recv, m_send, m_recv, mx_send, mx_recv,
    l_send, l_recv, p_send, p_recv, h_send, h_recv,
):
    g = lax.axis_index("grp")
    t = lax.axis_index("tok")
    n_x = lax.axis_size("grp") // 4
    n_g = lax.axis_size("grp")
    core = lax.rem(g, 2)
    pair = g - core
    x = lax.rem(g // 2, n_x)
    y_hi = g // (2 * n_x)
    y_lo = t // NZ
    z = lax.rem(t, NZ)
    swapped = core != y_lo
    head = core * NZ + z
    mate_grp = pair + y_lo
    far_grp = (1 - y_hi) * (2 * n_x) + x * 2 + y_lo
    mate_tok = head
    sib_grp = pair + 1 - core
    up_tok = y_lo * NZ + lax.rem(z + 1, NZ)
    down_tok = y_lo * NZ + lax.rem(z + NZ - 1, NZ)
    outer = g + 2 * core - 1
    has_outer = jnp.logical_and(outer >= 0, outer < n_g)

    early_loads = [
        pltpu.make_async_copy(src, dst, early_sem.at[n])
        for n, (src, dst) in enumerate(
            ((tok_hbm, tok_ref), (mod_hbm, mod_ref), (gate_hbm, gate_ref), (cb_hbm, cb_ref), (rb_hbm, rb_ref))
        )
    ]
    for load in early_loads:
        load.start()
    ext[...] = jnp.zeros_like(ext)

    barrier = pltpu.get_barrier_semaphore()

    def greet(grp, tok):
        pl.semaphore_signal(barrier, inc=1, device_id=(grp, tok), device_id_type=MESH)

    def greet_row(step, carry):
        other = lax.rem(t + step, FR)

        @pl.when(step > 0)
        def _():
            greet(g, other)

        greet(sib_grp, other)
        return carry

    lax.fori_loop(0, FR, greet_row, 0)
    for step in range(1, 4):
        beside = y_hi * (2 * n_x) + lax.rem(x + step, n_x) * 2 + core
        greet(beside, t)
        greet(beside, (1 - y_lo) * NZ + z)

    @pl.when(swapped)
    def _():
        greet(far_grp, mate_tok)

    @pl.when(has_outer)
    def _():
        greet(outer, t)

        @pl.when(t > 0)
        def _():
            greet(outer, t - 1)

        @pl.when(t < FR - 1)
        def _():
            greet(outer, t + 1)

    guests = 2 * FR - 1 + 6 + jnp.where(swapped, 1, 0) + jnp.where(
        has_outer, 1 + jnp.where(t > 0, 1, 0) + jnp.where(t < FR - 1, 1, 0), 0
    )

    load_lw = pltpu.make_async_copy(lw_hbm, lw, local_sem.at[0])
    load_ow = pltpu.make_async_copy(ow_hbm.at[core, :, x], ow, local_sem.at[1])
    load_cw = pltpu.make_async_copy(cw_hbm, cw, local_sem.at[2])
    load_rw = pltpu.make_async_copy(rw_hbm, rw, local_sem.at[3])
    load_lw.start()
    load_ow.start()

    def third(k):
        return wv.at[:, pl.ds(k * HD, HD)]

    def load_w(k):
        return pltpu.make_async_copy(w_hbm.at[k], third(k), wloc_sem.at[k])

    @pl.when(jnp.logical_not(swapped))
    def _():
        for k in range(3):
            load_w(k).start()

    load_cw.start()
    load_rw.start()

    def rows_of(sub):
        return pl.ds(sub * SUB, SUB)

    def swap_x(sub):
        return pltpu.make_async_remote_copy(
            src_ref=xown.at[rows_of(sub)],
            dst_ref=xall.at[t, rows_of(sub)],
            send_sem=swx_send.at[sub],
            recv_sem=swx_recv.at[sub],
            device_id=(mate_grp, mate_tok),
            device_id_type=MESH,
        )

    def wait_swap_x(sub):
        pltpu.make_async_copy(
            xall.at[head, rows_of(sub)], xall.at[head, rows_of(sub)], swx_recv.at[sub]
        ).wait()

    def swap_w(k):
        return pltpu.make_async_remote_copy(
            src_ref=w_hbm.at[k],
            dst_ref=third(k),
            send_sem=sww_send.at[k],
            recv_sem=sww_recv.at[k],
            device_id=(mate_grp if k == 2 else far_grp, mate_tok),
            device_id_type=MESH,
        )

    def swap_r():
        return pltpu.make_async_remote_copy(
            src_ref=rmine,
            dst_ref=rbuf,
            send_sem=swr_send.at[0],
            recv_sem=swr_recv.at[0],
            device_id=(mate_grp, mate_tok),
            device_id_type=MESH,
        )

    def ring(way, step, sub):
        origin = lax.rem(z + (NZ - step if way == 0 else step), NZ)
        block = xall.at[core * NZ + origin, rows_of(sub)]
        return pltpu.make_async_remote_copy(
            src_ref=block,
            dst_ref=block,
            send_sem=ring_send.at[way, step, sub],
            recv_sem=ring_recv.at[way, step, sub],
            device_id=(g, up_tok if way == 0 else down_tok),
            device_id_type=MESH,
        )

    def wait_ring(way, step, sub):
        origin = lax.rem(z + (NZ - step if way == 0 else step), NZ)
        block = xall.at[core * NZ + origin, rows_of(sub)]
        pltpu.make_async_copy(block, block, ring_recv.at[way, step - 1, sub]).wait()

    def share(origin, sub):
        block = xall.at[core * NZ + origin, rows_of(sub)]
        return pltpu.make_async_remote_copy(
            src_ref=block,
            dst_ref=block,
            send_sem=sib_send.at[origin, sub],
            recv_sem=sib_recv.at[origin, sub],
            device_id=(sib_grp, t),
            device_id_type=MESH,
        )

    def origin_of(way, step):
        return lax.rem(z + (NZ - step if way == 0 else step), NZ)

    reach = (4 - core, 3 + core)

    new = lax.broadcasted_iota(jnp.int32, (BLK, BLK), 0)
    old = lax.broadcasted_iota(jnp.int32, (BLK, BLK), 1)
    source = (lax.rem(new // 2, 4)) * 32 + (new // 8) * 2 + lax.rem(new, 2)
    pick = jnp.where(old == source, 1.0, 0.0).astype(BF16)

    def prepare(sub):
        own = jnp.dot(
            pick[sub * SUB : (sub + 1) * SUB], tok_ref[...], preferred_element_type=F32
        )
        scale = lax.rsqrt(jnp.mean(own * own, axis=-1, keepdims=True) + 1e-06)
        made = (own * scale * (1.0 + mod_ref[1:2, :]) + mod_ref[0:1, :]).astype(BF16)

        @pl.when(swapped)
        def _():
            xown[rows_of(sub), :] = made

        @pl.when(jnp.logical_not(swapped))
        def _():
            xall[head, rows_of(sub), :] = made

    def depart(sub):
        ring(0, 0, sub).start()
        ring(1, 0, sub).start()
        share(z, sub).start()

    for load in early_loads:
        load.wait()
    for sub in range(SUBS):
        prepare(sub)
        if sub == 0:
            pl.semaphore_wait(barrier, guests)

        @pl.when(swapped)
        def _():
            swap_x(sub).start()
            if sub < 2:
                swap_w(sub).start()

        @pl.when(jnp.logical_not(swapped))
        def _():
            depart(sub)

    load_lw.wait()
    own_rows = jnp.dot(pick, tok_ref[...], preferred_element_type=F32).astype(BF16)
    rmine[...] = jnp.dot(own_rows, lw[...], preferred_element_type=F32)

    @pl.when(swapped)
    def _():
        swap_w(2).start()
        swap_r().start()
        for sub in range(SUBS):
            wait_swap_x(sub)
            depart(sub)

    def fold_copy(other):
        return pltpu.make_async_remote_copy(
            src_ref=msend.at[lax.rem(other, NZ), pl.ds(pl.multiple_of(other // NZ * 16, 16), 16)],
            dst_ref=mrecv.at[t],
            send_sem=m_send.at[other],
            recv_sem=m_recv.at[t],
            device_id=(g, other),
            device_id_type=MESH,
        )

    def fold_wait(step, carry):
        other = lax.rem(t + step, FR)
        pltpu.make_async_copy(mrecv.at[other], mrecv.at[other], m_recv.at[other]).wait()
        return carry

    def fold_sent(step, carry):
        fold_copy(lax.rem(t + step, FR)).wait_send()
        return carry

    def fold_rows(which):
        return mfull.at[pl.ds(pl.multiple_of(which * 16, 16), 16)]

    share_no = x * 2 + y_lo

    def spread(step):
        there = lax.rem(share_no + step, 8)
        return pltpu.make_async_remote_copy(
            src_ref=fold_rows(share_no),
            dst_ref=fold_rows(share_no),
            send_sem=mx_send.at[step],
            recv_sem=mx_recv.at[share_no],
            device_id=(
                y_hi * (2 * n_x) + there // 2 * 2 + core,
                lax.rem(there, 2) * NZ + z,
            ),
            device_id_type=MESH,
        )

    def place_of(p):
        if isinstance(p, int):
            table = [(k, o) for k in (0, 1) for o in (0, 1, -1)]
            for far in (2, 3):
                table += [(k, o) for k in (0, 1) for o in (far, -far)]
            return (table + [(0, 4), (1, 4)])[p]
        stage, p = p
        if stage == 0:
            return p // 3, lax.rem(p + 1, 3) - 1
        if stage < 3:
            return (p - 4 * stage - 2) // 2, (stage + 1) * (1 - 2 * lax.rem(p, 2))
        return p - 14, 4

    def slot_of(p):
        kind, offset = place_of(p)
        return jnp.where(kind == 0, core, 1 - core) * NZ + lax.rem(z + NZ + offset, NZ)

    def project(stage, low, high):
        def one(p, carry):
            kind, offset = place_of((stage, p))
            origin = lax.rem(z + NZ + offset, NZ)

            @pl.when(kind == 1)
            def _():
                for sub in range(SUBS):
                    block = xall.at[(1 - core) * NZ + origin, rows_of(sub)]
                    pltpu.make_async_copy(block, block, sib_recv.at[origin, sub]).wait()

            triple = jnp.dot(xall[slot_of((stage, p))], wv[...], preferred_element_type=F32)
            qs[p] = (triple[:, :HD] * EXP_SCALE).astype(BF16)
            at = pl.ds(pl.multiple_of(p * BLK, BLK), BLK)
            kt[:, at] = triple[:, HD : 2 * HD].T.astype(BF16)
            v2[at, :HD] = triple[:, 2 * HD :].astype(BF16)
            return carry

        lax.fori_loop(low, high, one, 0)

    def forward(step, sub):
        for way in range(2):

            @pl.when(step <= reach[way])
            def _():
                wait_ring(way, step, sub)

                @pl.when(step < reach[way])
                def _():
                    ring(way, step, sub).start()

                share(origin_of(way, step), sub).start()

    def meet(query, low, high, before=None):
        keys = slice(low * BLK, high * BLK)
        scores = jnp.dot(query, kt[:, keys], preferred_element_type=F32)
        top = jnp.max(scores, axis=-1, keepdims=True)
        top = jnp.broadcast_to(top, (query.shape[0], HD))
        if before is not None:
            top = jnp.maximum(before, top)
        probs = jnp.exp2(scores - jnp.concatenate([top] * (high - low), axis=1))
        return top, jnp.dot(probs.astype(BF16), v2[keys, :], preferred_element_type=F32)

    def merged(summed, before, top, added):
        shrink = jnp.exp2(before - top)
        return summed * jnp.concatenate([shrink, shrink], axis=1) + added

    def fresh(low, high, upto):
        rows = (high - low) * BLK
        top, summed = meet(qs[low:high].reshape(rows, HD), 0, upto)
        tops[low:high] = top.reshape(high - low, BLK, HD)
        sums[low:high] = summed.reshape(high - low, BLK, 2 * HD)

    def update(count, low, high):
        rows = count * BLK
        before = tops[0:count].reshape(rows, HD)
        top, added = meet(qs[0:count].reshape(rows, HD), low, high, before)
        summed = merged(sums[0:count].reshape(rows, 2 * HD), before, top, added)
        tops[0:count] = top.reshape(count, BLK, HD)
        sums[0:count] = summed.reshape(count, BLK, 2 * HD)

    forward(1, 0)
    v2[:, HD:] = jnp.ones((v2.shape[0], HD), BF16)
    to = lax.broadcasted_iota(jnp.int32, (4 * BLK, 4 * BLK), 0)
    of = lax.broadcasted_iota(jnp.int32, (4 * BLK, 4 * BLK), 1)
    row, col = lax.rem(to // 4, 8), lax.rem(to, 4)
    phase = lax.rem(row, 2) * 2 + lax.rem(col, 2)
    order[...] = jnp.where(
        of == phase * BLK + (row // 2) * 32 + (col // 2) * FR + to // 32, 1.0, 0.0
    ).astype(BF16)

    forward(1, 1)
    load_ow.wait()
    scaled = (ow[...].astype(F32) * gate_ref[...]).astype(BF16).reshape(NZ * 32, 256)
    cols = pl.ds(pl.multiple_of(t * 256, 256), 256)
    part = jnp.dot(scaled, lw[cols, :], preferred_element_type=F32)
    msend[...] = part.astype(BF16).reshape(NZ, 32, LAT)

    mrecv[t] = msend[z, pl.ds(pl.multiple_of(y_lo * 16, 16), 16), :]

    def fold_send(step, carry):
        fold_copy(lax.rem(t + step, FR)).start()
        return carry

    lax.fori_loop(1, FR, fold_send, 0)

    forward(1, 2)

    load_rw.wait()
    taps = (((0,), (1, 2)), ((0, 1), (2,)))

    def combine(p, q):
        for a in range(3):
            for u in range(2):
                for v in range(2):
                    total = jnp.zeros((CH, CH), F32)
                    for b in taps[p][u]:
                        for c in taps[q][v]:
                            at = (b * 3 + c) * CH
                            total = total + rw[a, at : at + CH, :].astype(F32)
                    k = (u * 2 + v) * CH
                    wc[p * 2 + q, k : k + CH, a * CH : (a + 1) * CH] = total.astype(BF16)

    combine(0, 0)
    combine(0, 1)
    forward(1, 3)
    combine(1, 0)
    combine(1, 1)
    forward(2, 0)

    @pl.when(jnp.logical_not(swapped))
    def _():
        for k in range(3):
            load_w(k).wait()
        rbuf[...] = rmine[...]

    @pl.when(swapped)
    def _():
        for k in range(3):
            swap_w(k).wait_recv()
        pltpu.make_async_copy(rbuf, rbuf, swr_recv.at[0]).wait()

    project(0, 0, 2)
    forward(2, 1)
    project(0, 2, 4)
    forward(2, 2)
    project(0, 4, 6)
    forward(2, 3)
    fresh(0, 6, 6)

    forward(3, 0)
    project(1, 6, 8)
    lax.fori_loop(1, FR, fold_wait, 0)
    total = mrecv[0].astype(F32)
    for other in range(1, FR):
        total = total + mrecv[other].astype(F32)
    mfull[pl.ds(pl.multiple_of(share_no * 16, 16), 16), :] = total.astype(BF16)
    for step in range(1, 8):
        spread(step).start()
    forward(3, 1)
    project(1, 8, 10)
    forward(3, 2)
    update(6, 6, 10)
    forward(3, 3)
    fresh(6, 10, 10)

    forward(4, 0)
    project(2, 10, 12)
    forward(4, 1)
    project(2, 12, 14)
    forward(4, 2)
    update(10, 10, 14)
    fresh(10, 14, 14)
    for step in range(1, 8):
        there = lax.rem(share_no + step, 8)
        pltpu.make_async_copy(fold_rows(there), fold_rows(there), mx_recv.at[there]).wait()
    forward(4, 3)
    project(3, 14, 16)

    home = pair + y_lo

    def latent_copy(two):
        return pltpu.make_async_remote_copy(
            src_ref=lsend.at[two],
            dst_ref=lrecv.at[z],
            send_sem=l_send.at[two],
            recv_sem=l_recv.at[z],
            device_id=(home, two * 2 + core),
            device_id_type=MESH,
        )

    def to_sibling(two):
        return pltpu.make_async_remote_copy(
            src_ref=psend.at[two],
            dst_ref=precv.at[two],
            send_sem=p_send.at[two],
            recv_sem=p_recv.at[two],
            device_id=(sib_grp, t),
            device_id_type=MESH,
        )

    def is_self(two):
        return jnp.logical_and(home == g, two * 2 + core == t)

    def half_of(two, which):
        return lat[pl.ds(pl.multiple_of(two * 256 + which * BLK, BLK), BLK), :]

    H = BLK // 2

    def finish(half):
        part = pl.ds(half * H, H)
        before = tops[0:14, part].reshape(14 * H, HD)
        top, added = meet(qs[0:14, part].reshape(14 * H, HD), 14, 16, before)
        older = merged(sums[0:14, part].reshape(14 * H, 2 * HD), before, top, added)
        newer = meet(qs[14:16, part].reshape(2 * H, HD), 0, 16)[1]
        summed = jnp.concatenate([older, newer], axis=0)
        attended = (summed[:, :HD] / summed[:, HD:]).astype(BF16)
        latent = jnp.dot(attended, mfull[...], preferred_element_type=F32)
        for p in range(16):
            piece = latent[p * H : (p + 1) * H]
            if p == 0:
                piece = piece + rbuf[part, :]
            lat[pl.ds(slot_of(p) + half * H * FR, H, stride=FR), :] = piece

    def hand_over(n, carry):
        psend[n] = half_of(n, 1 - core).astype(BF16)
        to_sibling(n).start()
        return carry

    def pass_on(n, carry):
        two = (n // 4) * 4 + lax.rem(n + z, 4)
        to_sibling(two).wait_recv()
        summed = (half_of(two, core) + precv[two].astype(F32)).astype(BF16)

        @pl.when(jnp.logical_not(is_self(two)))
        def _():
            lsend[two] = summed
            latent_copy(two).start()

        @pl.when(is_self(two))
        def _():
            lrecv[z] = summed

        return carry

    for half in range(2):
        finish(half)
        lax.fori_loop(half * 4, half * 4 + 4, hand_over, 0)
        lax.fori_loop(half * 4, half * 4 + 4, pass_on, 0)

    def latent_wait(n, carry):
        here = jnp.logical_and(core == y_lo, lax.rem(t, 2) == core)

        @pl.when(jnp.logical_not(jnp.logical_and(here, n == z)))
        def _():
            pltpu.make_async_copy(lrecv.at[n], lrecv.at[n], l_recv.at[n]).wait()

        return carry

    lax.fori_loop(0, NZ, latent_wait, 0)
    tile = lrecv[0].astype(F32)
    for n in range(1, NZ):
        tile = tile + lrecv[n].astype(F32)
    ext[2:6, 2:4] = tile.astype(BF16).reshape(4, 2, FR, LAT)

    def halo(dg, dt):
        rows_src, rows_dst = {0: ((2, 4), (2, 4)), 1: ((4, 2), (0, 2)), -1: ((2, 2), (6, 2))}[dg]
        cols_dst = {0: 2, 1: 0, -1: 4}[dt]
        at = (dg + 1) * 3 + dt + 1
        return pltpu.make_async_remote_copy(
            src_ref=ext.at[pl.ds(*rows_src), pl.ds(2, 2)],
            dst_ref=ext.at[pl.ds(*rows_dst), pl.ds(cols_dst, 2)],
            send_sem=h_send.at[at],
            recv_sem=h_recv.at[at],
            device_id=(g + dg, t + dt),
            device_id_type=MESH,
        )

    def inside(dg, dt):
        ok = jnp.logical_and(g + dg >= 0, g + dg < n_g)
        return jnp.logical_and(ok, jnp.logical_and(t + dt >= 0, t + dt < FR))

    ways = [(dg, dt) for dg in (-1, 0, 1) for dt in (-1, 0, 1) if (dg, dt) != (0, 0)]
    for dg, dt in ways:

        @pl.when(inside(dg, dt))
        def _():
            halo(dg, dt).start()

    load_cw.wait()
    for dg, dt in ways:

        @pl.when(inside(-dg, -dt))
        def _():
            halo(dg, dt).wait_recv()

    def over_frames(three, rows):
        frame = lax.rem(lax.broadcasted_iota(jnp.int32, (rows, CH), 0), FR)
        before = pltpu.roll(three[0], 1, 0)
        after = pltpu.roll(three[2], rows - 1, 0)
        return (
            three[1]
            + jnp.where(frame > 0, before, 0.0)
            + jnp.where(frame < FR - 1, after, 0.0)
        )

    def silu(v):
        return v / (1.0 + jnp.exp(-v))

    views = [
        ext[b : b + 6, c : c + 4].reshape(24 * FR, LAT) for b in range(3) for c in range(3)
    ]
    cells = jnp.concatenate(views, axis=1)
    three = [jnp.dot(cells, cw[a], preferred_element_type=F32) for a in range(3)]
    made = silu(over_frames(three, 24 * FR) + cb_ref[...]).astype(BF16)
    coarse[...] = made.reshape(6, 4, FR, CH)

    @pl.when(g == 0)
    def _():
        coarse[0:1] = jnp.zeros((1, 4, FR, CH), BF16)

    @pl.when(g == n_g - 1)
    def _():
        coarse[5:6] = jnp.zeros((1, 4, FR, CH), BF16)

    @pl.when(t == 0)
    def _():
        coarse[:, 0:1] = jnp.zeros((6, 1, FR, CH), BF16)

    @pl.when(t == FR - 1)
    def _():
        coarse[:, 3:4] = jnp.zeros((6, 1, FR, CH), BF16)

    rows = 8 * FR
    parts = []
    for p in range(2):
        for q in range(2):
            views = [
                coarse[p + u : p + u + 4, q + v : q + v + 2].reshape(rows, CH)
                for u in range(2)
                for v in range(2)
            ]
            parts.append(
                jnp.dot(
                    jnp.concatenate(views, axis=1), wc[p * 2 + q], preferred_element_type=F32
                )
            )
    three = [
        jnp.concatenate([part[:, a * CH : (a + 1) * CH] for part in parts], axis=0)
        for a in range(3)
    ]
    mixed = over_frames(three, 4 * rows)
    center = coarse[1:5, 1:3].reshape(rows, CH).astype(F32)
    center = jnp.concatenate([center] * 4, axis=0)
    result = silu(center + mixed + rb_ref[...]).astype(BF16)
    out_ref[...] = jnp.dot(order[...], result, preferred_element_type=F32).astype(BF16)

    for sub in range(SUBS):

        @pl.when(swapped)
        def _():
            swap_x(sub).wait_send()

        for way in range(2):
            for step in range(4):

                @pl.when(step < reach[way])
                def _():
                    ring(way, step, sub).wait_send()

        for origin in range(NZ):
            share(origin, sub).wait_send()

    @pl.when(swapped)
    def _():
        for k in range(3):
            swap_w(k).wait_send()
        swap_r().wait_send()

    lax.fori_loop(1, FR, fold_sent, 0)
    for step in range(1, 8):
        spread(step).wait_send()

    def latent_sent(two, carry):
        to_sibling(two).wait_send()

        @pl.when(jnp.logical_not(is_self(two)))
        def _():
            latent_copy(two).wait_send()

        return carry

    lax.fori_loop(0, FR // 2, latent_sent, 0)
    for dg, dt in ways:

        @pl.when(inside(dg, dt))
        def _():
            halo(dg, dt).wait_send()


def shards(
    tokens,
    modulation,
    triple_weight,
    out_weight,
    gate,
    latent_weight,
    conv_weight,
    conv_bias,
    res_weight,
    res_bias,
):
    vmem = pl.BlockSpec(memory_space=pltpu.VMEM)
    hbm = pl.BlockSpec(memory_space=pl.ANY)
    dma = pltpu.SemaphoreType.DMA
    out = pl.pallas_call(
        kernel,
        out_shape=jax.ShapeDtypeStruct((4 * BLK, CH), BF16),
        in_specs=[hbm] * 10,
        out_specs=vmem,
        scratch_shapes=[
            pltpu.VMEM((BLK, D), BF16),
            pltpu.VMEM((2, D), F32),
            pltpu.VMEM((1, 256), F32),
            pltpu.VMEM((1, CH), F32),
            pltpu.VMEM((1, CH), F32),
            pltpu.VMEM((FR, BLK, D), BF16),
            pltpu.VMEM((BLK, D), BF16),
            pltpu.VMEM((D, 3 * HD), BF16),
            pltpu.VMEM((D, LAT), BF16),
            pltpu.VMEM((NZ, 32, 256), BF16),
            pltpu.VMEM((3, 9 * LAT, CH), BF16),
            pltpu.VMEM((3, 9 * CH, CH), BF16),
            pltpu.VMEM((FR, BLK, HD), BF16),
            pltpu.VMEM((HD, FR * BLK), BF16),
            pltpu.VMEM((FR * BLK, 2 * HD), BF16),
            pltpu.VMEM((BLK, LAT), F32),
            pltpu.VMEM((BLK, LAT), F32),
            pltpu.VMEM((FR, 16, LAT), BF16),
            pltpu.VMEM((NZ, 32, LAT), BF16),
            pltpu.VMEM((HD, LAT), BF16),
            pltpu.VMEM((NZ, BLK, LAT), BF16),
            pltpu.VMEM((NZ, BLK, LAT), BF16),
            pltpu.VMEM((NZ, BLK, LAT), BF16),
            pltpu.VMEM((NZ, BLK, LAT), BF16),
            pltpu.VMEM((FR * BLK, LAT), F32),
            pltpu.VMEM((FR, BLK, HD), F32),
            pltpu.VMEM((FR, BLK, 2 * HD), F32),
            pltpu.VMEM((4 * BLK, 4 * BLK), BF16),
            pltpu.VMEM((8, 6, FR, LAT), BF16),
            pltpu.VMEM((6, 4, FR, CH), BF16),
            pltpu.VMEM((4, 4 * CH, 3 * CH), BF16),
            dma((5,)),
            dma((4,)),
            dma((3,)),
            dma((SUBS,)), dma((SUBS,)),
            dma((3,)), dma((3,)),
            dma((1,)), dma((1,)),
            dma((2, 4, SUBS)), dma((2, 4, SUBS)),
            dma((NZ, SUBS)), dma((NZ, SUBS)),
            dma((FR,)), dma((FR,)),
            dma((8,)), dma((8,)),
            dma((NZ,)), dma((NZ,)),
            dma((NZ,)), dma((NZ,)),
            dma((9,)), dma((9,)),
        ],
        compiler_params=pltpu.CompilerParams(
            collective_id=0, has_side_effects=True, vmem_limit_bytes=60 * 2**20
        ),
        cost_estimate=pl.CostEstimate(
            flops=13 * 10**9, bytes_accessed=14 * 10**6, transcendentals=5 * 10**6
        ),
    )(
        tokens[0],
        modulation,
        triple_weight.transpose(1, 0, 2),
        out_weight.reshape(2, NZ, 4, 32, 256),
        gate.reshape(1, 256),
        latent_weight,
        conv_weight.reshape(3, 9 * LAT, CH),
        conv_bias.reshape(1, CH),
        res_weight.reshape(3, 9 * CH, CH),
        res_bias.reshape(1, CH),
    )
    return out.reshape(FR, 8, 4, CH)


def solution(mesh):
    placed = (
        P("grp", "tok", None),
        P(),
        P(None, None, "tok"),
        P(None, "tok"),
        P("tok"),
        P(),
        P(),
        P(),
        P(),
        P(),
    )
    return jax.shard_map(
        shards, mesh=mesh, in_specs=placed, out_specs=P(None, "grp", "tok", None), check_vma=False
    )
```

```python
import math

import jax
import jax.numpy as jnp
from jax import lax
from jax.experimental import pallas as pl
from jax.experimental.pallas import tpu as pltpu
from jax.sharding import PartitionSpec as P

MESH = pl.DeviceIdType.MESH
F32 = jnp.float32
BF16 = jnp.bfloat16

D = 4096
HD = 128
FR = 16
BLK = 128
SUBS = 4
SUB = BLK // SUBS
LAT = 128
CH = 256
NZ = 8
EXP_SCALE = HD ** (-0.5) * math.log2(math.e)


def kernel(
    tok_hbm, mod_hbm, w_hbm, ow_hbm, gate_hbm, lw_hbm, cw_hbm, cb_hbm, rw_hbm, rb_hbm,
    out_ref,
    tok_ref, mod_ref, gate_ref, cb_ref, rb_ref, xall, xown, wv, lw, ow, cw, rw, qs, kt, v2, rmine, rbuf, mrecv, msend, mfull,
    lsend, lrecv, psend, precv, lat, tops, sums, order, ext, coarse, wc,
    early_sem, local_sem, wloc_sem, swx_send, swx_recv, sww_send, sww_recv, swr_send, swr_recv,
    ring_send, ring_recv, sib_send, sib_recv, m_send, m_recv, mx_send, mx_recv,
    l_send, l_recv, p_send, p_recv, h_send, h_recv,
):
    g = lax.axis_index("grp")
    t = lax.axis_index("tok")
    n_x = lax.axis_size("grp") // 4
    n_g = lax.axis_size("grp")
    core = lax.rem(g, 2)
    pair = g - core
    x = lax.rem(g // 2, n_x)
    y_hi = g // (2 * n_x)
    y_lo = t // NZ
    z = lax.rem(t, NZ)
    swapped = core != y_lo
    head = core * NZ + z
    mate_grp = pair + y_lo
    far_grp = (1 - y_hi) * (2 * n_x) + x * 2 + y_lo
    mate_tok = head
    sib_grp = pair + 1 - core
    up_tok = y_lo * NZ + lax.rem(z + 1, NZ)
    down_tok = y_lo * NZ + lax.rem(z + NZ - 1, NZ)
    outer = g + 2 * core - 1
    has_outer = jnp.logical_and(outer >= 0, outer < n_g)

    early_loads = [
        pltpu.make_async_copy(src, dst, early_sem.at[n])
        for n, (src, dst) in enumerate(
            ((tok_hbm, tok_ref), (mod_hbm, mod_ref), (gate_hbm, gate_ref), (cb_hbm, cb_ref), (rb_hbm, rb_ref))
        )
    ]
    for load in early_loads:
        load.start()
    ext[...] = jnp.zeros_like(ext)

    barrier = pltpu.get_barrier_semaphore()

    def greet(grp, tok):
        pl.semaphore_signal(barrier, inc=1, device_id=(grp, tok), device_id_type=MESH)

    def greet_row(step, carry):
        other = lax.rem(t + step, FR)

        @pl.when(step > 0)
        def _():
            greet(g, other)

        greet(sib_grp, other)
        return carry

    lax.fori_loop(0, FR, greet_row, 0)
    for step in range(1, 4):
        beside = y_hi * (2 * n_x) + lax.rem(x + step, n_x) * 2 + core
        greet(beside, t)
        greet(beside, (1 - y_lo) * NZ + z)

    @pl.when(swapped)
    def _():
        greet(far_grp, mate_tok)

    @pl.when(has_outer)
    def _():
        greet(outer, t)

        @pl.when(t > 0)
        def _():
            greet(outer, t - 1)

        @pl.when(t < FR - 1)
        def _():
            greet(outer, t + 1)

    guests = 2 * FR - 1 + 6 + jnp.where(swapped, 1, 0) + jnp.where(
        has_outer, 1 + jnp.where(t > 0, 1, 0) + jnp.where(t < FR - 1, 1, 0), 0
    )

    load_lw = pltpu.make_async_copy(lw_hbm, lw, local_sem.at[0])
    load_ow = pltpu.make_async_copy(ow_hbm.at[core, :, x], ow, local_sem.at[1])
    load_cw = pltpu.make_async_copy(cw_hbm, cw, local_sem.at[2])
    load_rw = pltpu.make_async_copy(rw_hbm, rw, local_sem.at[3])
    load_lw.start()
    load_ow.start()

    def third(k):
        return wv.at[:, pl.ds(k * HD, HD)]

    def load_w(k):
        return pltpu.make_async_copy(w_hbm.at[k], third(k), wloc_sem.at[k])

    @pl.when(jnp.logical_not(swapped))
    def _():
        for k in range(3):
            load_w(k).start()

    load_cw.start()
    load_rw.start()

    def rows_of(sub):
        return pl.ds(sub * SUB, SUB)

    def swap_x(sub):
        return pltpu.make_async_remote_copy(
            src_ref=xown.at[rows_of(sub)],
            dst_ref=xall.at[t, rows_of(sub)],
            send_sem=swx_send.at[sub],
            recv_sem=swx_recv.at[sub],
            device_id=(mate_grp, mate_tok),
            device_id_type=MESH,
        )

    def wait_swap_x(sub):
        pltpu.make_async_copy(
            xall.at[head, rows_of(sub)], xall.at[head, rows_of(sub)], swx_recv.at[sub]
        ).wait()

    def swap_w(k):
        return pltpu.make_async_remote_copy(
            src_ref=w_hbm.at[k],
            dst_ref=third(k),
            send_sem=sww_send.at[k],
            recv_sem=sww_recv.at[k],
            device_id=(mate_grp if k == 2 else far_grp, mate_tok),
            device_id_type=MESH,
        )

    def swap_r():
        return pltpu.make_async_remote_copy(
            src_ref=rmine,
            dst_ref=rbuf,
            send_sem=swr_send.at[0],
            recv_sem=swr_recv.at[0],
            device_id=(mate_grp, mate_tok),
            device_id_type=MESH,
        )

    def ring(way, step, sub):
        origin = lax.rem(z + (NZ - step if way == 0 else step), NZ)
        block = xall.at[core * NZ + origin, rows_of(sub)]
        return pltpu.make_async_remote_copy(
            src_ref=block,
            dst_ref=block,
            send_sem=ring_send.at[way, step, sub],
            recv_sem=ring_recv.at[way, step, sub],
            device_id=(g, up_tok if way == 0 else down_tok),
            device_id_type=MESH,
        )

    def wait_ring(way, step, sub):
        origin = lax.rem(z + (NZ - step if way == 0 else step), NZ)
        block = xall.at[core * NZ + origin, rows_of(sub)]
        pltpu.make_async_copy(block, block, ring_recv.at[way, step - 1, sub]).wait()

    def share(origin, sub):
        block = xall.at[core * NZ + origin, rows_of(sub)]
        return pltpu.make_async_remote_copy(
            src_ref=block,
            dst_ref=block,
            send_sem=sib_send.at[origin, sub],
            recv_sem=sib_recv.at[origin, sub],
            device_id=(sib_grp, t),
            device_id_type=MESH,
        )

    def origin_of(way, step):
        return lax.rem(z + (NZ - step if way == 0 else step), NZ)

    reach = (4 - core, 3 + core)

    new = lax.broadcasted_iota(jnp.int32, (BLK, BLK), 0)
    old = lax.broadcasted_iota(jnp.int32, (BLK, BLK), 1)
    source = (lax.rem(new // 2, 4)) * 32 + (new // 8) * 2 + lax.rem(new, 2)
    pick = jnp.where(old == source, 1.0, 0.0).astype(BF16)

    def prepare(sub):
        own = jnp.dot(
            pick[sub * SUB : (sub + 1) * SUB], tok_ref[...], preferred_element_type=F32
        )
        scale = lax.rsqrt(jnp.mean(own * own, axis=-1, keepdims=True) + 1e-06)
        made = (own * scale * (1.0 + mod_ref[1:2, :]) + mod_ref[0:1, :]).astype(BF16)

        @pl.when(swapped)
        def _():
            xown[rows_of(sub), :] = made

        @pl.when(jnp.logical_not(swapped))
        def _():
            xall[head, rows_of(sub), :] = made

    def depart(sub):
        ring(0, 0, sub).start()
        ring(1, 0, sub).start()
        share(z, sub).start()

    for load in early_loads:
        load.wait()
    for sub in range(SUBS):
        prepare(sub)
        if sub == 0:
            pl.semaphore_wait(barrier, guests)

        @pl.when(swapped)
        def _():
            swap_x(sub).start()
            if sub < 2:
                swap_w(sub).start()

        @pl.when(jnp.logical_not(swapped))
        def _():
            depart(sub)

    load_lw.wait()
    own_rows = jnp.dot(pick, tok_ref[...], preferred_element_type=F32).astype(BF16)
    rmine[...] = jnp.dot(own_rows, lw[...], preferred_element_type=F32)

    @pl.when(swapped)
    def _():
        swap_w(2).start()
        swap_r().start()
        for sub in range(SUBS):
            wait_swap_x(sub)
            depart(sub)

    def fold_copy(other):
        return pltpu.make_async_remote_copy(
            src_ref=msend.at[lax.rem(other, NZ), pl.ds(pl.multiple_of(other // NZ * 16, 16), 16)],
            dst_ref=mrecv.at[t],
            send_sem=m_send.at[other],
            recv_sem=m_recv.at[t],
            device_id=(g, other),
            device_id_type=MESH,
        )

    def fold_wait(step, carry):
        other = lax.rem(t + step, FR)
        pltpu.make_async_copy(mrecv.at[other], mrecv.at[other], m_recv.at[other]).wait()
        return carry

    def fold_sent(step, carry):
        fold_copy(lax.rem(t + step, FR)).wait_send()
        return carry

    def fold_rows(which):
        return mfull.at[pl.ds(pl.multiple_of(which * 16, 16), 16)]

    share_no = x * 2 + y_lo

    def spread(step):
        there = lax.rem(share_no + step, 8)
        return pltpu.make_async_remote_copy(
            src_ref=fold_rows(share_no),
            dst_ref=fold_rows(share_no),
            send_sem=mx_send.at[step],
            recv_sem=mx_recv.at[share_no],
            device_id=(
                y_hi * (2 * n_x) + there // 2 * 2 + core,
                lax.rem(there, 2) * NZ + z,
            ),
            device_id_type=MESH,
        )

    def place_of(p):
        if isinstance(p, int):
            table = [(k, o) for k in (0, 1) for o in (0, 1, -1)]
            for far in (2, 3):
                table += [(k, o) for k in (0, 1) for o in (far, -far)]
            return (table + [(0, 4), (1, 4)])[p]
        stage, p = p
        if stage == 0:
            return p // 3, lax.rem(p + 1, 3) - 1
        if stage < 3:
            return (p - 4 * stage - 2) // 2, (stage + 1) * (1 - 2 * lax.rem(p, 2))
        return p - 14, 4

    def slot_of(p):
        kind, offset = place_of(p)
        return jnp.where(kind == 0, core, 1 - core) * NZ + lax.rem(z + NZ + offset, NZ)

    def project(stage, low, high):
        def one(p, carry):
            kind, offset = place_of((stage, p))
            origin = lax.rem(z + NZ + offset, NZ)

            @pl.when(kind == 1)
            def _():
                for sub in range(SUBS):
                    block = xall.at[(1 - core) * NZ + origin, rows_of(sub)]
                    pltpu.make_async_copy(block, block, sib_recv.at[origin, sub]).wait()

            triple = jnp.dot(xall[slot_of((stage, p))], wv[...], preferred_element_type=F32)
            qs[p] = (triple[:, :HD] * EXP_SCALE).astype(BF16)
            at = pl.ds(pl.multiple_of(p * BLK, BLK), BLK)
            kt[:, at] = triple[:, HD : 2 * HD].T.astype(BF16)
            v2[at, :HD] = triple[:, 2 * HD :].astype(BF16)
            return carry

        lax.fori_loop(low, high, one, 0)

    def forward(step, sub):
        for way in range(2):

            @pl.when(step <= reach[way])
            def _():
                wait_ring(way, step, sub)

                @pl.when(step < reach[way])
                def _():
                    ring(way, step, sub).start()

                share(origin_of(way, step), sub).start()

    def meet(query, low, high, before=None):
        keys = slice(low * BLK, high * BLK)
        scores = jnp.dot(query, kt[:, keys], preferred_element_type=F32)
        top = jnp.max(scores, axis=-1, keepdims=True)
        top = jnp.broadcast_to(top, (query.shape[0], HD))
        if before is not None:
            top = jnp.maximum(before, top)
        probs = jnp.exp2(scores - jnp.concatenate([top] * (high - low), axis=1))
        return top, jnp.dot(probs.astype(BF16), v2[keys, :], preferred_element_type=F32)

    def merged(summed, before, top, added):
        shrink = jnp.exp2(before - top)
        return summed * jnp.concatenate([shrink, shrink], axis=1) + added

    def fresh(low, high, upto):
        rows = (high - low) * BLK
        top, summed = meet(qs[low:high].reshape(rows, HD), 0, upto)
        tops[low:high] = top.reshape(high - low, BLK, HD)
        sums[low:high] = summed.reshape(high - low, BLK, 2 * HD)

    def update(count, low, high):
        rows = count * BLK
        before = tops[0:count].reshape(rows, HD)
        top, added = meet(qs[0:count].reshape(rows, HD), low, high, before)
        summed = merged(sums[0:count].reshape(rows, 2 * HD), before, top, added)
        tops[0:count] = top.reshape(count, BLK, HD)
        sums[0:count] = summed.reshape(count, BLK, 2 * HD)

    forward(1, 0)
    v2[:, HD:] = jnp.ones((v2.shape[0], HD), BF16)
    to = lax.broadcasted_iota(jnp.int32, (4 * BLK, 4 * BLK), 0)
    of = lax.broadcasted_iota(jnp.int32, (4 * BLK, 4 * BLK), 1)
    row, col = lax.rem(to // 4, 8), lax.rem(to, 4)
    phase = lax.rem(row, 2) * 2 + lax.rem(col, 2)
    order[...] = jnp.where(
        of == phase * BLK + (row // 2) * 32 + (col // 2) * FR + to // 32, 1.0, 0.0
    ).astype(BF16)

    forward(1, 1)
    load_ow.wait()
    scaled = (ow[...].astype(F32) * gate_ref[...]).astype(BF16).reshape(NZ * 32, 256)
    cols = pl.ds(pl.multiple_of(t * 256, 256), 256)
    part = jnp.dot(scaled, lw[cols, :], preferred_element_type=F32)
    msend[...] = part.astype(BF16).reshape(NZ, 32, LAT)

    mrecv[t] = msend[z, pl.ds(pl.multiple_of(y_lo * 16, 16), 16), :]

    def fold_send(step, carry):
        fold_copy(lax.rem(t + step, FR)).start()
        return carry

    lax.fori_loop(1, FR, fold_send, 0)

    forward(1, 2)

    load_rw.wait()
    taps = (((0,), (1, 2)), ((0, 1), (2,)))

    def combine(p, q):
        for a in range(3):
            for u in range(2):
                for v in range(2):
                    total = jnp.zeros((CH, CH), F32)
                    for b in taps[p][u]:
                        for c in taps[q][v]:
                            at = (b * 3 + c) * CH
                            total = total + rw[a, at : at + CH, :].astype(F32)
                    k = (u * 2 + v) * CH
                    wc[p * 2 + q, k : k + CH, a * CH : (a + 1) * CH] = total.astype(BF16)

    combine(0, 0)
    combine(0, 1)
    forward(1, 3)
    combine(1, 0)
    combine(1, 1)
    forward(2, 0)

    @pl.when(jnp.logical_not(swapped))
    def _():
        for k in range(3):
            load_w(k).wait()
        rbuf[...] = rmine[...]

    @pl.when(swapped)
    def _():
        for k in range(3):
            swap_w(k).wait_recv()
        pltpu.make_async_copy(rbuf, rbuf, swr_recv.at[0]).wait()

    project(0, 0, 2)
    forward(2, 1)
    project(0, 2, 4)
    forward(2, 2)
    project(0, 4, 6)
    forward(2, 3)
    fresh(0, 6, 6)

    forward(3, 0)
    project(1, 6, 8)
    lax.fori_loop(1, FR, fold_wait, 0)
    total = mrecv[0].astype(F32)
    for other in range(1, FR):
        total = total + mrecv[other].astype(F32)
    mfull[pl.ds(pl.multiple_of(share_no * 16, 16), 16), :] = total.astype(BF16)
    for step in range(1, 8):
        spread(step).start()
    forward(3, 1)
    project(1, 8, 10)
    forward(3, 2)
    update(6, 6, 10)
    forward(3, 3)
    fresh(6, 10, 10)

    forward(4, 0)
    project(2, 10, 12)
    project(2, 12, 14)
    update(10, 10, 14)
    fresh(10, 14, 14)
    forward(4, 1)
    forward(4, 2)
    for step in range(1, 8):
        there = lax.rem(share_no + step, 8)
        pltpu.make_async_copy(fold_rows(there), fold_rows(there), mx_recv.at[there]).wait()
    forward(4, 3)
    project(3, 14, 16)

    home = pair + y_lo

    def latent_copy(two):
        return pltpu.make_async_remote_copy(
            src_ref=lsend.at[two],
            dst_ref=lrecv.at[z],
            send_sem=l_send.at[two],
            recv_sem=l_recv.at[z],
            device_id=(home, two * 2 + core),
            device_id_type=MESH,
        )

    def to_sibling(two):
        return pltpu.make_async_remote_copy(
            src_ref=psend.at[two],
            dst_ref=precv.at[two],
            send_sem=p_send.at[two],
            recv_sem=p_recv.at[two],
            device_id=(sib_grp, t),
            device_id_type=MESH,
        )

    def is_self(two):
        return jnp.logical_and(home == g, two * 2 + core == t)

    def half_of(two, which):
        return lat[pl.ds(pl.multiple_of(two * 256 + which * BLK, BLK), BLK), :]

    H = BLK // 2

    def finish(half):
        part = pl.ds(half * H, H)
        before = tops[0:14, part].reshape(14 * H, HD)
        top, added = meet(qs[0:14, part].reshape(14 * H, HD), 14, 16, before)
        older = merged(sums[0:14, part].reshape(14 * H, 2 * HD), before, top, added)
        newer = meet(qs[14:16, part].reshape(2 * H, HD), 0, 16)[1]
        summed = jnp.concatenate([older, newer], axis=0)
        attended = (summed[:, :HD] / summed[:, HD:]).astype(BF16)
        latent = jnp.dot(attended, mfull[...], preferred_element_type=F32)
        for p in range(16):
            piece = latent[p * H : (p + 1) * H]
            if p == 0:
                piece = piece + rbuf[part, :]
            lat[pl.ds(slot_of(p) + half * H * FR, H, stride=FR), :] = piece

    def hand_over(n, carry):
        psend[n] = half_of(n, 1 - core).astype(BF16)
        to_sibling(n).start()
        return carry

    def pass_on(n, carry):
        two = (n // 4) * 4 + lax.rem(n + z, 4)
        to_sibling(two).wait_recv()
        summed = (half_of(two, core) + precv[two].astype(F32)).astype(BF16)

        @pl.when(jnp.logical_not(is_self(two)))
        def _():
            lsend[two] = summed
            latent_copy(two).start()

        @pl.when(is_self(two))
        def _():
            lrecv[z] = summed

        return carry

    for half in range(2):
        finish(half)
        lax.fori_loop(half * 4, half * 4 + 4, hand_over, 0)
        lax.fori_loop(half * 4, half * 4 + 4, pass_on, 0)

    for sub in range(SUBS):

        @pl.when(swapped)
        def _():
            swap_x(sub).wait_send()

        for way in range(2):
            for step in range(4):

                @pl.when(step < reach[way])
                def _():
                    ring(way, step, sub).wait_send()

        for origin in range(NZ):
            share(origin, sub).wait_send()

    @pl.when(swapped)
    def _():
        for k in range(3):
            swap_w(k).wait_send()
        swap_r().wait_send()

    lax.fori_loop(1, FR, fold_sent, 0)
    for step in range(1, 8):
        spread(step).wait_send()

    def latent_wait(n, carry):
        here = jnp.logical_and(core == y_lo, lax.rem(t, 2) == core)

        @pl.when(jnp.logical_not(jnp.logical_and(here, n == z)))
        def _():
            pltpu.make_async_copy(lrecv.at[n], lrecv.at[n], l_recv.at[n]).wait()

        return carry

    lax.fori_loop(0, NZ, latent_wait, 0)
    tile = lrecv[0].astype(F32)
    for n in range(1, NZ):
        tile = tile + lrecv[n].astype(F32)
    ext[2:6, 2:4] = tile.astype(BF16).reshape(4, 2, FR, LAT)

    def halo(dg, dt):
        rows_src, rows_dst = {0: ((2, 4), (2, 4)), 1: ((4, 2), (0, 2)), -1: ((2, 2), (6, 2))}[dg]
        cols_dst = {0: 2, 1: 0, -1: 4}[dt]
        at = (dg + 1) * 3 + dt + 1
        return pltpu.make_async_remote_copy(
            src_ref=ext.at[pl.ds(*rows_src), pl.ds(2, 2)],
            dst_ref=ext.at[pl.ds(*rows_dst), pl.ds(cols_dst, 2)],
            send_sem=h_send.at[at],
            recv_sem=h_recv.at[at],
            device_id=(g + dg, t + dt),
            device_id_type=MESH,
        )

    def inside(dg, dt):
        ok = jnp.logical_and(g + dg >= 0, g + dg < n_g)
        return jnp.logical_and(ok, jnp.logical_and(t + dt >= 0, t + dt < FR))

    ways = [(dg, dt) for dg in (-1, 0, 1) for dt in (-1, 0, 1) if (dg, dt) != (0, 0)]
    for dg, dt in ways:

        @pl.when(inside(dg, dt))
        def _():
            halo(dg, dt).start()

    def latent_sent(two, carry):
        to_sibling(two).wait_send()

        @pl.when(jnp.logical_not(is_self(two)))
        def _():
            latent_copy(two).wait_send()

        return carry

    lax.fori_loop(0, FR // 2, latent_sent, 0)
    load_cw.wait()
    for dg, dt in ways:

        @pl.when(inside(-dg, -dt))
        def _():
            halo(dg, dt).wait_recv()

    def over_frames(three, rows):
        frame = lax.rem(lax.broadcasted_iota(jnp.int32, (rows, CH), 0), FR)
        before = pltpu.roll(three[0], 1, 0)
        after = pltpu.roll(three[2], rows - 1, 0)
        return (
            three[1]
            + jnp.where(frame > 0, before, 0.0)
            + jnp.where(frame < FR - 1, after, 0.0)
        )

    def silu(v):
        return v / (1.0 + jnp.exp(-v))

    views = [
        ext[b : b + 6, c : c + 4].reshape(24 * FR, LAT) for b in range(3) for c in range(3)
    ]
    cells = jnp.concatenate(views, axis=1)
    three = [jnp.dot(cells, cw[a], preferred_element_type=F32) for a in range(3)]
    made = silu(over_frames(three, 24 * FR) + cb_ref[...]).astype(BF16)
    coarse[...] = made.reshape(6, 4, FR, CH)

    @pl.when(g == 0)
    def _():
        coarse[0:1] = jnp.zeros((1, 4, FR, CH), BF16)

    @pl.when(g == n_g - 1)
    def _():
        coarse[5:6] = jnp.zeros((1, 4, FR, CH), BF16)

    @pl.when(t == 0)
    def _():
        coarse[:, 0:1] = jnp.zeros((6, 1, FR, CH), BF16)

    @pl.when(t == FR - 1)
    def _():
        coarse[:, 3:4] = jnp.zeros((6, 1, FR, CH), BF16)

    rows = 8 * FR
    parts = []
    for p in range(2):
        for q in range(2):
            views = [
                coarse[p + u : p + u + 4, q + v : q + v + 2].reshape(rows, CH)
                for u in range(2)
                for v in range(2)
            ]
            parts.append(
                jnp.dot(
                    jnp.concatenate(views, axis=1), wc[p * 2 + q], preferred_element_type=F32
                )
            )
    three = [
        jnp.concatenate([part[:, a * CH : (a + 1) * CH] for part in parts], axis=0)
        for a in range(3)
    ]
    mixed = over_frames(three, 4 * rows)
    center = coarse[1:5, 1:3].reshape(rows, CH).astype(F32)
    center = jnp.concatenate([center] * 4, axis=0)
    result = silu(center + mixed + rb_ref[...]).astype(BF16)
    out_ref[...] = jnp.dot(order[...], result, preferred_element_type=F32).astype(BF16)

    for dg, dt in ways:

        @pl.when(inside(dg, dt))
        def _():
            halo(dg, dt).wait_send()


def shards(
    tokens,
    modulation,
    triple_weight,
    out_weight,
    gate,
    latent_weight,
    conv_weight,
    conv_bias,
    res_weight,
    res_bias,
):
    vmem = pl.BlockSpec(memory_space=pltpu.VMEM)
    hbm = pl.BlockSpec(memory_space=pl.ANY)
    dma = pltpu.SemaphoreType.DMA
    out = pl.pallas_call(
        kernel,
        out_shape=jax.ShapeDtypeStruct((4 * BLK, CH), BF16),
        in_specs=[hbm] * 10,
        out_specs=vmem,
        scratch_shapes=[
            pltpu.VMEM((BLK, D), BF16),
            pltpu.VMEM((2, D), F32),
            pltpu.VMEM((1, 256), F32),
            pltpu.VMEM((1, CH), F32),
            pltpu.VMEM((1, CH), F32),
            pltpu.VMEM((FR, BLK, D), BF16),
            pltpu.VMEM((BLK, D), BF16),
            pltpu.VMEM((D, 3 * HD), BF16),
            pltpu.VMEM((D, LAT), BF16),
            pltpu.VMEM((NZ, 32, 256), BF16),
            pltpu.VMEM((3, 9 * LAT, CH), BF16),
            pltpu.VMEM((3, 9 * CH, CH), BF16),
            pltpu.VMEM((FR, BLK, HD), BF16),
            pltpu.VMEM((HD, FR * BLK), BF16),
            pltpu.VMEM((FR * BLK, 2 * HD), BF16),
            pltpu.VMEM((BLK, LAT), F32),
            pltpu.VMEM((BLK, LAT), F32),
            pltpu.VMEM((FR, 16, LAT), BF16),
            pltpu.VMEM((NZ, 32, LAT), BF16),
            pltpu.VMEM((HD, LAT), BF16),
            pltpu.VMEM((NZ, BLK, LAT), BF16),
            pltpu.VMEM((NZ, BLK, LAT), BF16),
            pltpu.VMEM((NZ, BLK, LAT), BF16),
            pltpu.VMEM((NZ, BLK, LAT), BF16),
            pltpu.VMEM((FR * BLK, LAT), F32),
            pltpu.VMEM((FR, BLK, HD), F32),
            pltpu.VMEM((FR, BLK, 2 * HD), F32),
            pltpu.VMEM((4 * BLK, 4 * BLK), BF16),
            pltpu.VMEM((8, 6, FR, LAT), BF16),
            pltpu.VMEM((6, 4, FR, CH), BF16),
            pltpu.VMEM((4, 4 * CH, 3 * CH), BF16),
            dma((5,)),
            dma((4,)),
            dma((3,)),
            dma((SUBS,)), dma((SUBS,)),
            dma((3,)), dma((3,)),
            dma((1,)), dma((1,)),
            dma((2, 4, SUBS)), dma((2, 4, SUBS)),
            dma((NZ, SUBS)), dma((NZ, SUBS)),
            dma((FR,)), dma((FR,)),
            dma((8,)), dma((8,)),
            dma((NZ,)), dma((NZ,)),
            dma((NZ,)), dma((NZ,)),
            dma((9,)), dma((9,)),
        ],
        compiler_params=pltpu.CompilerParams(
            collective_id=0, has_side_effects=True, vmem_limit_bytes=60 * 2**20
        ),
        cost_estimate=pl.CostEstimate(
            flops=13 * 10**9, bytes_accessed=14 * 10**6, transcendentals=5 * 10**6
        ),
    )(
        tokens[0],
        modulation,
        triple_weight.transpose(1, 0, 2),
        out_weight.reshape(2, NZ, 4, 32, 256),
        gate.reshape(1, 256),
        latent_weight,
        conv_weight.reshape(3, 9 * LAT, CH),
        conv_bias.reshape(1, CH),
        res_weight.reshape(3, 9 * CH, CH),
        res_bias.reshape(1, CH),
    )
    return out.reshape(FR, 8, 4, CH)


def solution(mesh):
    placed = (
        P("grp", "tok", None),
        P(),
        P(None, None, "tok"),
        P(None, "tok"),
        P("tok"),
        P(),
        P(),
        P(),
        P(),
        P(),
    )
    return jax.shard_map(
        shards, mesh=mesh, in_specs=placed, out_specs=P(None, "grp", "tok", None), check_vma=False
    )
```

```python
import math

import jax
import jax.numpy as jnp
from jax import lax
from jax.experimental import pallas as pl
from jax.experimental.pallas import tpu as pltpu
from jax.sharding import PartitionSpec as P

MESH = pl.DeviceIdType.MESH
F32 = jnp.float32
BF16 = jnp.bfloat16

D = 4096
HD = 128
FR = 16
BLK = 128
SUBS = 4
SUB = BLK // SUBS
LAT = 128
CH = 256
NZ = 8
EXP_SCALE = HD ** (-0.5) * math.log2(math.e)


def kernel(
    tok_hbm, mod_hbm, w_hbm, ow_hbm, gate_hbm, lw_hbm, cw_hbm, cb_hbm, rw_hbm, rb_hbm,
    out_ref,
    tok_ref, mod_ref, gate_ref, cb_ref, rb_ref, xall, xown, wv, lw, ow, cw, rw, qs, kt, v2, rmine, rbuf, mrecv, msend, mfull,
    lsend, lrecv, psend, precv, lat, tops, sums, order, ext, coarse, wc,
    early_sem, local_sem, wloc_sem, swx_send, swx_recv, sww_send, sww_recv, swr_send, swr_recv,
    ring_send, ring_recv, sib_send, sib_recv, m_send, m_recv, mx_send, mx_recv,
    l_send, l_recv, p_send, p_recv, h_send, h_recv,
):
    g = lax.axis_index("grp")
    t = lax.axis_index("tok")
    n_x = lax.axis_size("grp") // 4
    n_g = lax.axis_size("grp")
    core = lax.rem(g, 2)
    pair = g - core
    x = lax.rem(g // 2, n_x)
    y_hi = g // (2 * n_x)
    y_lo = t // NZ
    z = lax.rem(t, NZ)
    swapped = core != y_lo
    head = core * NZ + z
    mate_grp = pair + y_lo
    far_grp = (1 - y_hi) * (2 * n_x) + x * 2 + y_lo
    mate_tok = head
    sib_grp = pair + 1 - core
    up_tok = y_lo * NZ + lax.rem(z + 1, NZ)
    down_tok = y_lo * NZ + lax.rem(z + NZ - 1, NZ)
    outer = g + 2 * core - 1
    has_outer = jnp.logical_and(outer >= 0, outer < n_g)

    early_loads = [
        pltpu.make_async_copy(src, dst, early_sem.at[n])
        for n, (src, dst) in enumerate(
            ((tok_hbm, tok_ref), (mod_hbm, mod_ref), (gate_hbm, gate_ref), (cb_hbm, cb_ref), (rb_hbm, rb_ref))
        )
    ]
    for load in early_loads:
        load.start()
    ext[...] = jnp.zeros_like(ext)

    barrier = pltpu.get_barrier_semaphore()

    def greet(grp, tok):
        pl.semaphore_signal(barrier, inc=1, device_id=(grp, tok), device_id_type=MESH)

    def greet_row(step, carry):
        other = lax.rem(t + step, FR)

        @pl.when(step > 0)
        def _():
            greet(g, other)

        greet(sib_grp, other)
        return carry

    lax.fori_loop(0, FR, greet_row, 0)
    for step in range(1, 4):
        beside = y_hi * (2 * n_x) + lax.rem(x + step, n_x) * 2 + core
        greet(beside, t)
        greet(beside, (1 - y_lo) * NZ + z)

    @pl.when(swapped)
    def _():
        greet(far_grp, mate_tok)

    @pl.when(has_outer)
    def _():
        greet(outer, t)

        @pl.when(t > 0)
        def _():
            greet(outer, t - 1)

        @pl.when(t < FR - 1)
        def _():
            greet(outer, t + 1)

    guests = 2 * FR - 1 + 6 + jnp.where(swapped, 1, 0) + jnp.where(
        has_outer, 1 + jnp.where(t > 0, 1, 0) + jnp.where(t < FR - 1, 1, 0), 0
    )

    load_lw = pltpu.make_async_copy(lw_hbm, lw, local_sem.at[0])
    load_ow = pltpu.make_async_copy(ow_hbm.at[core, :, x], ow, local_sem.at[1])
    load_cw = pltpu.make_async_copy(cw_hbm, cw, local_sem.at[2])
    load_rw = pltpu.make_async_copy(rw_hbm, rw, local_sem.at[3])
    load_lw.start()
    load_ow.start()

    def third(k):
        return wv.at[:, pl.ds(k * HD, HD)]

    def load_w(k):
        return pltpu.make_async_copy(w_hbm.at[k], third(k), wloc_sem.at[k])

    @pl.when(jnp.logical_not(swapped))
    def _():
        for k in range(3):
            load_w(k).start()

    load_cw.start()
    load_rw.start()

    def rows_of(sub):
        return pl.ds(sub * SUB, SUB)

    def swap_x(sub):
        return pltpu.make_async_remote_copy(
            src_ref=xown.at[rows_of(sub)],
            dst_ref=xall.at[t, rows_of(sub)],
            send_sem=swx_send.at[sub],
            recv_sem=swx_recv.at[sub],
            device_id=(mate_grp, mate_tok),
            device_id_type=MESH,
        )

    def wait_swap_x(sub):
        pltpu.make_async_copy(
            xall.at[head, rows_of(sub)], xall.at[head, rows_of(sub)], swx_recv.at[sub]
        ).wait()

    def swap_w(k):
        return pltpu.make_async_remote_copy(
            src_ref=w_hbm.at[k],
            dst_ref=third(k),
            send_sem=sww_send.at[k],
            recv_sem=sww_recv.at[k],
            device_id=(mate_grp if k == 2 else far_grp, mate_tok),
            device_id_type=MESH,
        )

    def swap_r():
        return pltpu.make_async_remote_copy(
            src_ref=rmine,
            dst_ref=rbuf,
            send_sem=swr_send.at[0],
            recv_sem=swr_recv.at[0],
            device_id=(mate_grp, mate_tok),
            device_id_type=MESH,
        )

    def ring(way, step, sub):
        origin = lax.rem(z + (NZ - step if way == 0 else step), NZ)
        block = xall.at[core * NZ + origin, rows_of(sub)]
        return pltpu.make_async_remote_copy(
            src_ref=block,
            dst_ref=block,
            send_sem=ring_send.at[way, step, sub],
            recv_sem=ring_recv.at[way, step, sub],
            device_id=(g, up_tok if way == 0 else down_tok),
            device_id_type=MESH,
        )

    def wait_ring(way, step, sub):
        origin = lax.rem(z + (NZ - step if way == 0 else step), NZ)
        block = xall.at[core * NZ + origin, rows_of(sub)]
        pltpu.make_async_copy(block, block, ring_recv.at[way, step - 1, sub]).wait()

    def share(origin, sub):
        block = xall.at[core * NZ + origin, rows_of(sub)]
        return pltpu.make_async_remote_copy(
            src_ref=block,
            dst_ref=block,
            send_sem=sib_send.at[origin, sub],
            recv_sem=sib_recv.at[origin, sub],
            device_id=(sib_grp, t),
            device_id_type=MESH,
        )

    def origin_of(way, step):
        return lax.rem(z + (NZ - step if way == 0 else step), NZ)

    reach = (4 - core, 3 + core)

    new = lax.broadcasted_iota(jnp.int32, (BLK, BLK), 0)
    old = lax.broadcasted_iota(jnp.int32, (BLK, BLK), 1)
    source = (lax.rem(new // 2, 4)) * 32 + (new // 8) * 2 + lax.rem(new, 2)
    pick = jnp.where(old == source, 1.0, 0.0).astype(BF16)

    def prepare(sub):
        own = jnp.dot(
            pick[sub * SUB : (sub + 1) * SUB], tok_ref[...], preferred_element_type=F32
        )
        scale = lax.rsqrt(jnp.mean(own * own, axis=-1, keepdims=True) + 1e-06)
        made = (own * scale * (1.0 + mod_ref[1:2, :]) + mod_ref[0:1, :]).astype(BF16)

        @pl.when(swapped)
        def _():
            xown[rows_of(sub), :] = made

        @pl.when(jnp.logical_not(swapped))
        def _():
            xall[head, rows_of(sub), :] = made

    def depart(sub):
        ring(0, 0, sub).start()
        ring(1, 0, sub).start()
        share(z, sub).start()

    for load in early_loads:
        load.wait()
    for sub in range(SUBS):
        prepare(sub)
        if sub == 0:
            pl.semaphore_wait(barrier, guests)

        @pl.when(swapped)
        def _():
            swap_x(sub).start()
            if sub < 2:
                swap_w(sub).start()

        @pl.when(jnp.logical_not(swapped))
        def _():
            depart(sub)

    @pl.when(swapped)
    def _():
        swap_w(2).start()
        for sub in range(SUBS):
            wait_swap_x(sub)
            depart(sub)

    load_lw.wait()
    own_rows = jnp.dot(pick, tok_ref[...], preferred_element_type=F32).astype(BF16)
    rmine[...] = jnp.dot(own_rows, lw[...], preferred_element_type=F32)

    @pl.when(swapped)
    def _():
        swap_r().start()

    def fold_copy(other):
        return pltpu.make_async_remote_copy(
            src_ref=msend.at[lax.rem(other, NZ), pl.ds(pl.multiple_of(other // NZ * 16, 16), 16)],
            dst_ref=mrecv.at[t],
            send_sem=m_send.at[other],
            recv_sem=m_recv.at[t],
            device_id=(g, other),
            device_id_type=MESH,
        )

    def fold_wait(step, carry):
        other = lax.rem(t + step, FR)
        pltpu.make_async_copy(mrecv.at[other], mrecv.at[other], m_recv.at[other]).wait()
        return carry

    def fold_sent(step, carry):
        fold_copy(lax.rem(t + step, FR)).wait_send()
        return carry

    def fold_rows(which):
        return mfull.at[pl.ds(pl.multiple_of(which * 16, 16), 16)]

    share_no = x * 2 + y_lo

    def spread(step):
        there = lax.rem(share_no + step, 8)
        return pltpu.make_async_remote_copy(
            src_ref=fold_rows(share_no),
            dst_ref=fold_rows(share_no),
            send_sem=mx_send.at[step],
            recv_sem=mx_recv.at[share_no],
            device_id=(
                y_hi * (2 * n_x) + there // 2 * 2 + core,
                lax.rem(there, 2) * NZ + z,
            ),
            device_id_type=MESH,
        )

    def place_of(p):
        if isinstance(p, int):
            table = [(k, o) for k in (0, 1) for o in (0, 1, -1)]
            for far in (2, 3):
                table += [(k, o) for k in (0, 1) for o in (far, -far)]
            return (table + [(0, 4), (1, 4)])[p]
        stage, p = p
        if stage == 0:
            return p // 3, lax.rem(p + 1, 3) - 1
        if stage < 3:
            return (p - 4 * stage - 2) // 2, (stage + 1) * (1 - 2 * lax.rem(p, 2))
        return p - 14, 4

    def slot_of(p):
        kind, offset = place_of(p)
        return jnp.where(kind == 0, core, 1 - core) * NZ + lax.rem(z + NZ + offset, NZ)

    def project(stage, low, high):
        def one(p, carry):
            kind, offset = place_of((stage, p))
            origin = lax.rem(z + NZ + offset, NZ)

            @pl.when(kind == 1)
            def _():
                for sub in range(SUBS):
                    block = xall.at[(1 - core) * NZ + origin, rows_of(sub)]
                    pltpu.make_async_copy(block, block, sib_recv.at[origin, sub]).wait()

            triple = jnp.dot(xall[slot_of((stage, p))], wv[...], preferred_element_type=F32)
            qs[p] = (triple[:, :HD] * EXP_SCALE).astype(BF16)
            at = pl.ds(pl.multiple_of(p * BLK, BLK), BLK)
            kt[:, at] = triple[:, HD : 2 * HD].T.astype(BF16)
            v2[at, :HD] = triple[:, 2 * HD :].astype(BF16)
            return carry

        lax.fori_loop(low, high, one, 0)

    def forward(step, sub):
        for way in range(2):

            @pl.when(step <= reach[way])
            def _():
                wait_ring(way, step, sub)

                @pl.when(step < reach[way])
                def _():
                    ring(way, step, sub).start()

                share(origin_of(way, step), sub).start()

    def meet(query, low, high, before=None):
        keys = slice(low * BLK, high * BLK)
        scores = jnp.dot(query, kt[:, keys], preferred_element_type=F32)
        top = jnp.max(scores, axis=-1, keepdims=True)
        top = jnp.broadcast_to(top, (query.shape[0], HD))
        if before is not None:
            top = jnp.maximum(before, top)
        probs = jnp.exp2(scores - jnp.concatenate([top] * (high - low), axis=1))
        return top, jnp.dot(probs.astype(BF16), v2[keys, :], preferred_element_type=F32)

    def merged(summed, before, top, added):
        shrink = jnp.exp2(before - top)
        return summed * jnp.concatenate([shrink, shrink], axis=1) + added

    def fresh(low, high, upto):
        rows = (high - low) * BLK
        top, summed = meet(qs[low:high].reshape(rows, HD), 0, upto)
        tops[low:high] = top.reshape(high - low, BLK, HD)
        sums[low:high] = summed.reshape(high - low, BLK, 2 * HD)

    def update(count, low, high):
        rows = count * BLK
        before = tops[0:count].reshape(rows, HD)
        top, added = meet(qs[0:count].reshape(rows, HD), low, high, before)
        summed = merged(sums[0:count].reshape(rows, 2 * HD), before, top, added)
        tops[0:count] = top.reshape(count, BLK, HD)
        sums[0:count] = summed.reshape(count, BLK, 2 * HD)

    forward(1, 0)
    v2[:, HD:] = jnp.ones((v2.shape[0], HD), BF16)
    to = lax.broadcasted_iota(jnp.int32, (4 * BLK, 4 * BLK), 0)
    of = lax.broadcasted_iota(jnp.int32, (4 * BLK, 4 * BLK), 1)
    row, col = lax.rem(to // 4, 8), lax.rem(to, 4)
    phase = lax.rem(row, 2) * 2 + lax.rem(col, 2)
    order[...] = jnp.where(
        of == phase * BLK + (row // 2) * 32 + (col // 2) * FR + to // 32, 1.0, 0.0
    ).astype(BF16)

    forward(1, 1)
    load_ow.wait()
    scaled = (ow[...].astype(F32) * gate_ref[...]).astype(BF16).reshape(NZ * 32, 256)
    cols = pl.ds(pl.multiple_of(t * 256, 256), 256)
    part = jnp.dot(scaled, lw[cols, :], preferred_element_type=F32)
    msend[...] = part.astype(BF16).reshape(NZ, 32, LAT)

    mrecv[t] = msend[z, pl.ds(pl.multiple_of(y_lo * 16, 16), 16), :]

    def fold_send(step, carry):
        fold_copy(lax.rem(t + step, FR)).start()
        return carry

    lax.fori_loop(1, FR, fold_send, 0)

    forward(1, 2)

    load_rw.wait()
    taps = (((0,), (1, 2)), ((0, 1), (2,)))

    def combine(p, q):
        for a in range(3):
            for u in range(2):
                for v in range(2):
                    total = jnp.zeros((CH, CH), F32)
                    for b in taps[p][u]:
                        for c in taps[q][v]:
                            at = (b * 3 + c) * CH
                            total = total + rw[a, at : at + CH, :].astype(F32)
                    k = (u * 2 + v) * CH
                    wc[p * 2 + q, k : k + CH, a * CH : (a + 1) * CH] = total.astype(BF16)

    combine(0, 0)
    combine(0, 1)
    forward(1, 3)
    combine(1, 0)
    combine(1, 1)
    forward(2, 0)

    @pl.when(jnp.logical_not(swapped))
    def _():
        for k in range(3):
            load_w(k).wait()
        rbuf[...] = rmine[...]

    @pl.when(swapped)
    def _():
        for k in range(3):
            swap_w(k).wait_recv()
        pltpu.make_async_copy(rbuf, rbuf, swr_recv.at[0]).wait()

    project(0, 0, 2)
    forward(2, 1)
    project(0, 2, 4)
    forward(2, 2)
    project(0, 4, 6)
    forward(2, 3)
    fresh(0, 6, 6)

    forward(3, 0)
    project(1, 6, 8)
    lax.fori_loop(1, FR, fold_wait, 0)
    total = mrecv[0].astype(F32)
    for other in range(1, FR):
        total = total + mrecv[other].astype(F32)
    mfull[pl.ds(pl.multiple_of(share_no * 16, 16), 16), :] = total.astype(BF16)
    for step in range(1, 8):
        spread(step).start()
    forward(3, 1)
    project(1, 8, 10)
    forward(3, 2)
    update(6, 6, 10)
    forward(3, 3)
    fresh(6, 10, 10)

    forward(4, 0)
    project(2, 10, 12)
    project(2, 12, 14)
    update(10, 10, 14)
    fresh(10, 14, 14)
    forward(4, 1)
    forward(4, 2)
    for step in range(1, 8):
        there = lax.rem(share_no + step, 8)
        pltpu.make_async_copy(fold_rows(there), fold_rows(there), mx_recv.at[there]).wait()
    forward(4, 3)
    project(3, 14, 16)

    home = pair + y_lo

    def latent_copy(two):
        return pltpu.make_async_remote_copy(
            src_ref=lsend.at[two],
            dst_ref=lrecv.at[z],
            send_sem=l_send.at[two],
            recv_sem=l_recv.at[z],
            device_id=(home, two * 2 + core),
            device_id_type=MESH,
        )

    def to_sibling(two):
        return pltpu.make_async_remote_copy(
            src_ref=psend.at[two],
            dst_ref=precv.at[two],
            send_sem=p_send.at[two],
            recv_sem=p_recv.at[two],
            device_id=(sib_grp, t),
            device_id_type=MESH,
        )

    def is_self(two):
        return jnp.logical_and(home == g, two * 2 + core == t)

    def half_of(two, which):
        return lat[pl.ds(pl.multiple_of(two * 256 + which * BLK, BLK), BLK), :]

    H = BLK // 2

    def finish(half):
        part = pl.ds(half * H, H)
        before = tops[0:14, part].reshape(14 * H, HD)
        top, added = meet(qs[0:14, part].reshape(14 * H, HD), 14, 16, before)
        older = merged(sums[0:14, part].reshape(14 * H, 2 * HD), before, top, added)
        newer = meet(qs[14:16, part].reshape(2 * H, HD), 0, 16)[1]
        summed = jnp.concatenate([older, newer], axis=0)
        attended = (summed[:, :HD] / summed[:, HD:]).astype(BF16)
        latent = jnp.dot(attended, mfull[...], preferred_element_type=F32)
        for p in range(16):
            piece = latent[p * H : (p + 1) * H]
            if p == 0:
                piece = piece + rbuf[part, :]
            lat[pl.ds(slot_of(p) + half * H * FR, H, stride=FR), :] = piece

    def hand_over(n, carry):
        psend[n] = half_of(n, 1 - core).astype(BF16)
        to_sibling(n).start()
        return carry

    def pass_on(n, carry):
        two = (n // 4) * 4 + lax.rem(n + z, 4)
        to_sibling(two).wait_recv()
        summed = (half_of(two, core) + precv[two].astype(F32)).astype(BF16)

        @pl.when(jnp.logical_not(is_self(two)))
        def _():
            lsend[two] = summed
            latent_copy(two).start()

        @pl.when(is_self(two))
        def _():
            lrecv[z] = summed

        return carry

    for half in range(2):
        finish(half)
        lax.fori_loop(half * 4, half * 4 + 4, hand_over, 0)
        lax.fori_loop(half * 4, half * 4 + 4, pass_on, 0)

    for sub in range(SUBS):

        @pl.when(swapped)
        def _():
            swap_x(sub).wait_send()

        for way in range(2):
            for step in range(4):

                @pl.when(step < reach[way])
                def _():
                    ring(way, step, sub).wait_send()

        for origin in range(NZ):
            share(origin, sub).wait_send()

    @pl.when(swapped)
    def _():
        for k in range(3):
            swap_w(k).wait_send()
        swap_r().wait_send()

    lax.fori_loop(1, FR, fold_sent, 0)
    for step in range(1, 8):
        spread(step).wait_send()

    def latent_wait(n, carry):
        here = jnp.logical_and(core == y_lo, lax.rem(t, 2) == core)

        @pl.when(jnp.logical_not(jnp.logical_and(here, n == z)))
        def _():
            pltpu.make_async_copy(lrecv.at[n], lrecv.at[n], l_recv.at[n]).wait()

        return carry

    lax.fori_loop(0, NZ, latent_wait, 0)
    tile = lrecv[0].astype(F32)
    for n in range(1, NZ):
        tile = tile + lrecv[n].astype(F32)
    ext[2:6, 2:4] = tile.astype(BF16).reshape(4, 2, FR, LAT)

    def halo(dg, dt):
        rows_src, rows_dst = {0: ((2, 4), (2, 4)), 1: ((4, 2), (0, 2)), -1: ((2, 2), (6, 2))}[dg]
        cols_dst = {0: 2, 1: 0, -1: 4}[dt]
        at = (dg + 1) * 3 + dt + 1
        return pltpu.make_async_remote_copy(
            src_ref=ext.at[pl.ds(*rows_src), pl.ds(2, 2)],
            dst_ref=ext.at[pl.ds(*rows_dst), pl.ds(cols_dst, 2)],
            send_sem=h_send.at[at],
            recv_sem=h_recv.at[at],
            device_id=(g + dg, t + dt),
            device_id_type=MESH,
        )

    def inside(dg, dt):
        ok = jnp.logical_and(g + dg >= 0, g + dg < n_g)
        return jnp.logical_and(ok, jnp.logical_and(t + dt >= 0, t + dt < FR))

    ways = [(dg, dt) for dg in (-1, 0, 1) for dt in (-1, 0, 1) if (dg, dt) != (0, 0)]
    for dg, dt in ways:

        @pl.when(inside(dg, dt))
        def _():
            halo(dg, dt).start()

    def latent_sent(two, carry):
        to_sibling(two).wait_send()

        @pl.when(jnp.logical_not(is_self(two)))
        def _():
            latent_copy(two).wait_send()

        return carry

    lax.fori_loop(0, FR // 2, latent_sent, 0)
    load_cw.wait()
    for dg, dt in ways:

        @pl.when(inside(-dg, -dt))
        def _():
            halo(dg, dt).wait_recv()

    def over_frames(three, rows):
        frame = lax.rem(lax.broadcasted_iota(jnp.int32, (rows, CH), 0), FR)
        before = pltpu.roll(three[0], 1, 0)
        after = pltpu.roll(three[2], rows - 1, 0)
        return (
            three[1]
            + jnp.where(frame > 0, before, 0.0)
            + jnp.where(frame < FR - 1, after, 0.0)
        )

    def silu(v):
        return v / (1.0 + jnp.exp(-v))

    views = [
        ext[b : b + 6, c : c + 4].reshape(24 * FR, LAT) for b in range(3) for c in range(3)
    ]
    cells = jnp.concatenate(views, axis=1)
    three = [jnp.dot(cells, cw[a], preferred_element_type=F32) for a in range(3)]
    made = silu(over_frames(three, 24 * FR) + cb_ref[...]).astype(BF16)
    coarse[...] = made.reshape(6, 4, FR, CH)

    @pl.when(g == 0)
    def _():
        coarse[0:1] = jnp.zeros((1, 4, FR, CH), BF16)

    @pl.when(g == n_g - 1)
    def _():
        coarse[5:6] = jnp.zeros((1, 4, FR, CH), BF16)

    @pl.when(t == 0)
    def _():
        coarse[:, 0:1] = jnp.zeros((6, 1, FR, CH), BF16)

    @pl.when(t == FR - 1)
    def _():
        coarse[:, 3:4] = jnp.zeros((6, 1, FR, CH), BF16)

    rows = 8 * FR
    parts = []
    for p in range(2):
        for q in range(2):
            views = [
                coarse[p + u : p + u + 4, q + v : q + v + 2].reshape(rows, CH)
                for u in range(2)
                for v in range(2)
            ]
            parts.append(
                jnp.dot(
                    jnp.concatenate(views, axis=1), wc[p * 2 + q], preferred_element_type=F32
                )
            )
    three = [
        jnp.concatenate([part[:, a * CH : (a + 1) * CH] for part in parts], axis=0)
        for a in range(3)
    ]
    mixed = over_frames(three, 4 * rows)
    center = coarse[1:5, 1:3].reshape(rows, CH).astype(F32)
    center = jnp.concatenate([center] * 4, axis=0)
    result = silu(center + mixed + rb_ref[...]).astype(BF16)
    out_ref[...] = jnp.dot(order[...], result, preferred_element_type=F32).astype(BF16)

    for dg, dt in ways:

        @pl.when(inside(dg, dt))
        def _():
            halo(dg, dt).wait_send()


def shards(
    tokens,
    modulation,
    triple_weight,
    out_weight,
    gate,
    latent_weight,
    conv_weight,
    conv_bias,
    res_weight,
    res_bias,
):
    vmem = pl.BlockSpec(memory_space=pltpu.VMEM)
    hbm = pl.BlockSpec(memory_space=pl.ANY)
    dma = pltpu.SemaphoreType.DMA
    out = pl.pallas_call(
        kernel,
        out_shape=jax.ShapeDtypeStruct((4 * BLK, CH), BF16),
        in_specs=[hbm] * 10,
        out_specs=vmem,
        scratch_shapes=[
            pltpu.VMEM((BLK, D), BF16),
            pltpu.VMEM((2, D), F32),
            pltpu.VMEM((1, 256), F32),
            pltpu.VMEM((1, CH), F32),
            pltpu.VMEM((1, CH), F32),
            pltpu.VMEM((FR, BLK, D), BF16),
            pltpu.VMEM((BLK, D), BF16),
            pltpu.VMEM((D, 3 * HD), BF16),
            pltpu.VMEM((D, LAT), BF16),
            pltpu.VMEM((NZ, 32, 256), BF16),
            pltpu.VMEM((3, 9 * LAT, CH), BF16),
            pltpu.VMEM((3, 9 * CH, CH), BF16),
            pltpu.VMEM((FR, BLK, HD), BF16),
            pltpu.VMEM((HD, FR * BLK), BF16),
            pltpu.VMEM((FR * BLK, 2 * HD), BF16),
            pltpu.VMEM((BLK, LAT), F32),
            pltpu.VMEM((BLK, LAT), F32),
            pltpu.VMEM((FR, 16, LAT), BF16),
            pltpu.VMEM((NZ, 32, LAT), BF16),
            pltpu.VMEM((HD, LAT), BF16),
            pltpu.VMEM((NZ, BLK, LAT), BF16),
            pltpu.VMEM((NZ, BLK, LAT), BF16),
            pltpu.VMEM((NZ, BLK, LAT), BF16),
            pltpu.VMEM((NZ, BLK, LAT), BF16),
            pltpu.VMEM((FR * BLK, LAT), F32),
            pltpu.VMEM((FR, BLK, HD), F32),
            pltpu.VMEM((FR, BLK, 2 * HD), F32),
            pltpu.VMEM((4 * BLK, 4 * BLK), BF16),
            pltpu.VMEM((8, 6, FR, LAT), BF16),
            pltpu.VMEM((6, 4, FR, CH), BF16),
            pltpu.VMEM((4, 4 * CH, 3 * CH), BF16),
            dma((5,)),
            dma((4,)),
            dma((3,)),
            dma((SUBS,)), dma((SUBS,)),
            dma((3,)), dma((3,)),
            dma((1,)), dma((1,)),
            dma((2, 4, SUBS)), dma((2, 4, SUBS)),
            dma((NZ, SUBS)), dma((NZ, SUBS)),
            dma((FR,)), dma((FR,)),
            dma((8,)), dma((8,)),
            dma((NZ,)), dma((NZ,)),
            dma((NZ,)), dma((NZ,)),
            dma((9,)), dma((9,)),
        ],
        compiler_params=pltpu.CompilerParams(
            collective_id=0, has_side_effects=True, vmem_limit_bytes=60 * 2**20
        ),
        cost_estimate=pl.CostEstimate(
            flops=13 * 10**9, bytes_accessed=14 * 10**6, transcendentals=5 * 10**6
        ),
    )(
        tokens[0],
        modulation,
        triple_weight.transpose(1, 0, 2),
        out_weight.reshape(2, NZ, 4, 32, 256),
        gate.reshape(1, 256),
        latent_weight,
        conv_weight.reshape(3, 9 * LAT, CH),
        conv_bias.reshape(1, CH),
        res_weight.reshape(3, 9 * CH, CH),
        res_bias.reshape(1, CH),
    )
    return out.reshape(FR, 8, 4, CH)


def solution(mesh):
    placed = (
        P("grp", "tok", None),
        P(),
        P(None, None, "tok"),
        P(None, "tok"),
        P("tok"),
        P(),
        P(),
        P(),
        P(),
        P(),
    )
    return jax.shard_map(
        shards, mesh=mesh, in_specs=placed, out_specs=P(None, "grp", "tok", None), check_vma=False
    )
```
